128 devices in a mesh: gx: 8 (over z, core), gy: 16 (over x, y).
Axes of the slice: x: 4, y: 4, z: 4, core: 2. Of those that a mesh axis runs over, the one named last changes fastest.
Arguments:
- features: bfloat16 [131072, 512], P(('gx', 'gy')), may hold values from -6 to 6
- weight: bfloat16 [512, 512], replicated, may hold values from -0.25 to 0.25
- attn_src: float32 [512], replicated, may hold values from -0.6 to 0.6
- attn_dst: float32 [512], replicated, may hold values from -0.6 to 0.6
- upstream: bfloat16 [131072, 512], P(('gx', 'gy')), may hold values from -6 to 6
- scores: float32 [131072, 80], P(('gx', 'gy')), may hold values from -8 to 300
- neighbour_lists: int32 [1024, 16], P(('gx', 'gy')), may hold values from 0 to 1023, as said below
- edge_index: int32 [131072, 80], P(('gx', 'gy')), may hold values from 0 to 2047, as said below
Outputs:
- grad_features: bfloat16 [131072, 512], P(('gx', 'gy'))
- grad_weight: float32 [512, 512], replicated
- grad_src: float32 [512], replicated
- grad_dst: float32 [512], replicated
The draws below stay inside these ranges and needn't reach their ends.
Inputs may be any that keep to these rules, and one draw needn't show every extreme that they name: `neighbour_lists`: blocks are numbered device by device in mesh order, 8 to a device. The list of block b names 16 different blocks, all held by devices whose gx and gy indices are within one of b's device's (wrapping around both axes); the first entry is b itself. `edge_index`: the 80 entries of one node are different.
All inputs are finite; a program needn't handle non-finite values.
Results may differ from the reference program's by a relative error of at most 0.0057.
Values may be sent and summed in bfloat16 or wider, within the bound.
No kernel may reach another device: no remote copies, remote signals or barrier semaphores. Data moves between devices by JAX's collectives and lax.ppermute only.
A program may use at most 128 MiB of HBM per device.

```python
import jax
import jax.numpy as jnp
from jax import lax

D = 512
F = 512
BLK = 128
NBL = 16
K = 80
NB_DEV = 8
NBLK = 1024
NODES = 131072
N_GX = 8
N_GY = 16


def draw_scores(key, part):
    key = jax.random.fold_in(key, 11)
    keys = jax.random.split(key, 1)
    base = 2.0 * jax.random.normal(keys[0], (NODES, K), jnp.float32)
    return jnp.clip(base, -8.0, 8.0)


def draw_neighbour_lists(key, part):
    key = jax.random.fold_in(key, 12)
    count = 9 * NB_DEV
    node_block = jnp.arange(NBLK, dtype=jnp.int32)[:, None]
    device = node_block // NB_DEV
    home_x = device // N_GY
    home_y = device % N_GY
    local = node_block % NB_DEV
    cand = jnp.arange(count, dtype=jnp.int32)[None, :]
    off_x = cand // (3 * NB_DEV)
    off_y = cand // NB_DEV % 3
    cand_local = cand % NB_DEV
    target = ((home_x + off_x - 1) % N_GX * N_GY + (home_y + off_y - 1) % N_GY) * NB_DEV + cand_local
    noise = jax.random.randint(key, (NBLK, count), 0, 1 << 20)
    rank = noise * count + cand
    selfish = cand == 4 * NB_DEV + local
    rank = jnp.where(selfish, (1 << 20) * count + count, rank)
    _, picked = lax.top_k(rank, NBL)
    return jnp.take_along_axis(target, picked, axis=1).astype(jnp.int32)


def draw_edge_index(key, part):
    key = jax.random.fold_in(key, 13)
    block_width = NBL * BLK
    ceiling = (1 << 30) // block_width
    noise = jax.random.randint(key, (NODES, block_width), 0, ceiling)
    rank = noise * block_width + jnp.arange(block_width, dtype=jnp.int32)[None, :]
    _, picked = lax.top_k(rank, K)
    return picked.astype(jnp.int32)


def level_of(own_key, dims, shards, least, largest):
    loudness = 1.0
    for dim, parts in shards:
        draws = jax.random.uniform(jax.random.fold_in(jax.random.fold_in(own_key, 6), dim), (parts,), jnp.float32, least / len(shards), largest / len(shards))
        loudness = loudness * jnp.repeat(jnp.exp(draws), dims[dim] // parts).reshape((-1,) + (1,) * (len(dims) - 1 - dim))
    return loudness


def normal_values(own_key, extent, scale, bound, shards=(), kind=jnp.bfloat16):
    level = level_of(own_key, extent, shards, -0.22, 0.18) if shards else 1.0
    drawn = jax.random.normal(own_key, extent, jnp.float32) * scale * level
    return jnp.minimum(jnp.maximum(drawn, -bound), bound).astype(kind)


def setup_inputs(seed: int = 0) -> dict:
    splits = jax.random.split(jax.random.key(seed), 9)
    return {
        "features": normal_values(splits[0], (NODES, D), 1.0, 6.0, ((0, 128),)),
        "weight": normal_values(splits[1], (D, F), D ** -0.5, 0.25),
        "attn_src": normal_values(splits[2], (F,), 0.1, 0.6, (), jnp.float32),
        "attn_dst": normal_values(splits[3], (F,), 0.1, 0.6, (), jnp.float32),
        "upstream": normal_values(splits[4], (NODES, F), 1.0, 6.0, ((0, 128),)),
        "scores": draw_scores(jax.random.fold_in(splits[8], 71), 0),
        "neighbour_lists": draw_neighbour_lists(jax.random.fold_in(splits[8], 71), 0),
        "edge_index": draw_edge_index(jax.random.fold_in(splits[8], 71), 0),
    }


def reference(features, weight, attn_src, attn_dst, upstream, scores, neighbour_lists, edge_index):
    projected = jnp.dot(features, weight, preferred_element_type=jnp.float32).astype(jnp.bfloat16)
    grad_up = upstream.reshape(NBLK, BLK, F)
    score_blocks = scores.reshape(NBLK, BLK, K)
    index_blocks = edge_index.reshape(NBLK, BLK, K)
    own_blocks = projected.reshape(NBLK, BLK, F)

    def step(carry, item):
        grad_acc, dst_acc, src_acc = carry
        lists, grad_blk, score_blk, index_blk, own_blk = item
        neighbour = lists[index_blk // BLK] * BLK + index_blk % BLK
        gathered = projected[neighbour].astype(jnp.float32)
        dalpha = jnp.einsum('if,ikf->ik', grad_blk.astype(jnp.float32), gathered)
        logit = jnp.where(score_blk > 0, score_blk, 0.2 * score_blk)
        alpha = jax.nn.softmax(logit, axis=1)
        inner = lax.optimization_barrier(jnp.sum(alpha * dalpha, axis=1, keepdims=True))
        dz = alpha * (dalpha - inner) * jnp.where(score_blk > 0, 1.0, 0.2)
        du = lax.optimization_barrier(jnp.sum(dz, axis=1))
        alpha_low = lax.optimization_barrier(alpha.astype(jnp.bfloat16)).astype(jnp.float32)
        contrib = alpha_low[:, :, None] * grad_blk.astype(jnp.float32)[:, None, :] + dz[:, :, None] * attn_dst[None, None, :]
        grad_acc = grad_acc.at[neighbour].add(contrib)
        dst_acc = dst_acc + jnp.einsum('ik,ikf->f', dz, gathered)
        src_acc = src_acc + jnp.dot(du, own_blk.astype(jnp.float32))
        return ((grad_acc, dst_acc, src_acc), du)
    start = (jnp.zeros((NODES, F), jnp.float32), jnp.zeros((F,), jnp.float32), jnp.zeros((F,), jnp.float32))
    (grad_acc, dst_acc, src_acc), du_all = lax.scan(step, start, (neighbour_lists, grad_up, score_blocks, index_blocks, own_blocks))
    grad_proj = grad_acc + du_all.reshape(NODES)[:, None] * attn_src[None, :]
    grad_low = grad_proj.astype(jnp.bfloat16)
    grad_features = jnp.dot(grad_low, weight.T, preferred_element_type=jnp.float32).astype(jnp.bfloat16)
    scale = 1.0 / jnp.sqrt(jnp.float32(NODES))
    grad_weight = jnp.dot(features.T, grad_low, preferred_element_type=jnp.float32) * scale
    return (grad_features, grad_weight, src_acc * scale, dst_acc * scale)
```

```python
import functools
import math

import jax
import jax.numpy as jnp
from jax import lax
from jax.experimental import pallas as pl
from jax.experimental.pallas import tpu as pltpu
from jax.sharding import PartitionSpec as P

BLK = 128
NBL = 16
WIDE = 256
HALVES = NBL * BLK // WIDE
LANES = 128
MIB = 1 << 20

f32 = jnp.float32
bf16 = jnp.bfloat16


def spread_body(blocks, edges, slots, score_ref, index_ref, grad_ref, dense_ref, own_ref, core_ref,
                far_ref, hi_scr, lo_scr, main_scr, rest_scr, grad_t, left_scr, right_scr, acc):
    step = pl.program_id(0)
    per = 3 * blocks

    @pl.when(step == 0)
    def _():
        own_ref[...] = jnp.zeros_like(own_ref)
        acc[...] = jnp.zeros_like(acc)
        hi_scr[...] = jnp.full_like(hi_scr, -1)
        lo_scr[...] = jnp.zeros_like(lo_scr)
        main_scr[...] = jnp.zeros_like(main_scr)
        rest_scr[...] = jnp.zeros_like(rest_scr)

    score = score_ref[...]
    logit = jnp.where(score > 0, score, 0.2 * score)
    expo = jnp.exp(logit - jnp.max(logit, axis=1, keepdims=True))
    alpha = expo / jnp.sum(expo, axis=1, keepdims=True)
    main = alpha.astype(bf16).astype(f32)
    rest = (alpha - main).astype(bf16).astype(f32)
    main_scr[:, 0:edges] = jnp.where(score > 0, main, -main)
    rest_scr[:, 0:edges] = jnp.where(score > 0, rest, -rest)
    index = index_ref[...]
    hi_scr[:, 0:edges] = index // WIDE
    lo_scr[:, 0:edges] = (index % WIDE).astype(f32)
    lo_scr[...] = lo_scr[...].T
    grad_t[...] = grad_ref[...].T

    wide_iota = lax.broadcasted_iota(jnp.int32, (edges, WIDE), 1).astype(f32).astype(bf16)
    half_iota = lax.broadcasted_iota(jnp.int32, (HALVES, LANES), 0)
    one = jnp.ones((edges, WIDE), bf16)
    none = jnp.zeros((edges, WIDE), bf16)
    tail = jnp.zeros((LANES - edges, WIDE), bf16)

    def group(g, carry):
        base = pl.multiple_of(g * 8, 8)
        cols = pltpu.roll(lo_scr[0:edges, :], LANES - base, 1).astype(bf16)
        hi = hi_scr[pl.ds(base, 8), :]
        main_g = main_scr[pl.ds(base, 8), :]
        rest_g = rest_scr[pl.ds(base, 8), :]
        for j in range(8):
            here = jnp.broadcast_to(hi[j:j + 1, :], (HALVES, LANES)) == half_iota
            lhs = jnp.concatenate(
                [
                    jnp.where(here, jnp.broadcast_to(main_g[j:j + 1, :], (HALVES, LANES)), 0.0),
                    jnp.where(here, jnp.broadcast_to(rest_g[j:j + 1, :], (HALVES, LANES)), 0.0),
                ],
                axis=0,
            ).astype(bf16)
            col = jnp.broadcast_to(cols[:, j:j + 1], (edges, WIDE))
            rhs = jnp.concatenate([jnp.where(col == wide_iota, one, none), tail], axis=0)
            out = jnp.dot(lhs, rhs, preferred_element_type=f32)
            where = pl.ds(pl.multiple_of((base + j) * 16, 16), 16)
            left_scr[where, :] = out[:, :LANES]
            right_scr[where, :] = out[:, LANES:]
        return carry

    lax.fori_loop(0, BLK // 8, group, 0)

    for h in range(HALVES):
        main_h = jnp.concatenate([r[pl.ds(h, BLK, stride=16), :] for r in (left_scr, right_scr)], axis=1)
        rest_h = jnp.concatenate([r[pl.ds(HALVES + h, BLK, stride=16), :] for r in (left_scr, right_scr)], axis=1)
        dense_ref[0, :, h * WIDE:(h + 1) * WIDE] = main_h + rest_h
        contrib = jnp.dot(grad_t[...], jnp.abs(main_h).astype(bf16), preferred_element_type=f32)
        for part in range(2):
            slot = slots[step, 2 * h + part]
            piece = contrib[:, part * BLK:(part + 1) * BLK]

            @pl.when(slot < per)
            def _():
                own_ref[pl.ds(slot, 1)] += piece[None]

            @pl.when(slot >= per)
            def _():
                acc[pl.ds(slot - per, 1)] += piece[None]

    @pl.when(step == pl.num_programs(0) - 1)
    def _():
        def cast(k, carry):
            core_ref[pl.ds(k, 1)] = acc[pl.ds(k, 1)].astype(bf16)
            far_ref[pl.ds(k, 1)] = acc[pl.ds(per + k, 1)].astype(bf16)
            return carry

        lax.fori_loop(0, per, cast, 0)


def spread(slots, scores, index, grad):
    rows, edges = scores.shape
    width = grad.shape[1]
    blocks = rows // BLK
    per = 3 * blocks
    whole = lambda: pl.BlockSpec((per, width, BLK), lambda b, s: (0, 0, 0), pipeline_mode=pl.Buffered(1))
    return pl.pallas_call(
        functools.partial(spread_body, blocks, edges),
        grid_spec=pltpu.PrefetchScalarGridSpec(
            num_scalar_prefetch=1,
            grid=(blocks,),
            in_specs=[
                pl.BlockSpec((BLK, edges), lambda b, s: (b, 0)),
                pl.BlockSpec((BLK, edges), lambda b, s: (b, 0)),
                pl.BlockSpec((BLK, width), lambda b, s: (b, 0)),
            ],
            out_specs=[
                pl.BlockSpec((1, BLK, NBL * BLK), lambda b, s: (b, 0, 0)),
                whole(), whole(), whole(),
            ],
            scratch_shapes=[
                pltpu.VMEM((BLK, LANES), jnp.int32),
                pltpu.VMEM((BLK, LANES), f32),
                pltpu.VMEM((BLK, LANES), f32),
                pltpu.VMEM((BLK, LANES), f32),
                pltpu.VMEM((width, BLK), bf16),
                pltpu.VMEM((BLK * 16, LANES), f32),
                pltpu.VMEM((BLK * 16, LANES), f32),
                pltpu.VMEM((2 * per, width, BLK), f32),
            ],
        ),
        out_shape=[
            jax.ShapeDtypeStruct((blocks, BLK, NBL * BLK), f32),
            jax.ShapeDtypeStruct((per, width, BLK), f32),
            jax.ShapeDtypeStruct((per, width, BLK), bf16),
            jax.ShapeDtypeStruct((per, width, BLK), bf16),
        ],
        compiler_params=pltpu.CompilerParams(
            dimension_semantics=("arbitrary",), vmem_limit_bytes=56 * MIB
        ),
        cost_estimate=pl.CostEstimate(
            flops=20 * 10**9, bytes_accessed=24 * MIB, transcendentals=rows * LANES
        ),
        name="spread",
    )(slots, scores, index, grad)


def softmax_grad_body(blocks, slots, dense_ref, probe_ref, *rest):
    tables = rest[:9]
    sums_ref, du_ref, vec_ref, table, prod, sem = rest[9:]
    step = pl.program_id(0)
    width = vec_ref.shape[1]

    @pl.when(step == 0)
    def _():
        copies = [
            pltpu.make_async_copy(t, table.at[pl.ds(k * blocks, blocks)], sem.at[k])
            for k, t in enumerate(tables)
        ]
        for copy in copies:
            copy.start()
        sums_ref[...] = jnp.zeros_like(sums_ref)
        for copy in copies:
            copy.wait()

    inner = jnp.zeros((BLK, BLK), f32)
    total = jnp.zeros((BLK, BLK), f32)
    for s in range(NBL):
        cols = slice(s * BLK, (s + 1) * BLK)
        cand = table[slots[step, s]]
        d = lax.dot_general(
            probe_ref[...], cand, (((1,), (1,)), ((), ())), preferred_element_type=f32
        )
        prod[:, cols] = d
        a = jnp.abs(dense_ref[0, :, cols])
        inner = inner + a * d
        total = total + a
    mean = jnp.sum(inner, axis=1, keepdims=True) / jnp.sum(total, axis=1, keepdims=True)
    du = jnp.zeros((BLK, BLK), f32)
    for s in range(NBL):
        cols = slice(s * BLK, (s + 1) * BLK)
        a = dense_ref[0, :, cols]
        dz = jnp.where(a > 0, a, -0.2 * a) * (prod[:, cols] - mean)
        du = du + dz
        slot = slots[step, s]
        sums_ref[pl.ds(slot, 1)] += jnp.sum(dz, axis=0, keepdims=True)[None]
    row = jnp.broadcast_to(jnp.sum(du, axis=1, keepdims=True), (BLK, BLK)).T
    du_ref[pl.ds(step, 1)] = row[0:1, :][None]

    @pl.when(step == pl.num_programs(0) - 1)
    def _():
        sub = lax.broadcasted_iota(jnp.int32, (16, BLK), 0)

        def two_rows(row):
            row = jnp.broadcast_to(row, (16, BLK))
            main = row.astype(bf16).astype(f32)
            both = jnp.where(sub == 0, main, jnp.where(sub == 1, row - main, 0.0))
            return both.astype(bf16)

        def product(ref, first):
            lhs = jnp.concatenate([two_rows(ref[first + k]) for k in range(blocks)], axis=1)
            rhs = table[pl.ds(first, blocks)].reshape(blocks * BLK, width)
            out = jnp.dot(lhs, rhs, preferred_element_type=f32)
            return out[0:1, :] + out[1:2, :]

        vec_ref[0:1, :] = product(du_ref, 0)
        vec_ref[1:2, :] = lax.fori_loop(
            0, 9, lambda k, v: v + product(sums_ref, pl.multiple_of(k * blocks, blocks)),
            jnp.zeros((1, width), f32),
        )


def softmax_grad(slots, dense, probe, tables):
    blocks = dense.shape[0]
    width = probe.shape[1]
    count = 9 * blocks
    return pl.pallas_call(
        functools.partial(softmax_grad_body, blocks),
        grid_spec=pltpu.PrefetchScalarGridSpec(
            num_scalar_prefetch=1,
            grid=(blocks,),
            in_specs=[
                pl.BlockSpec((1, BLK, NBL * BLK), lambda b, s: (b, 0, 0)),
                pl.BlockSpec((BLK, width), lambda b, s: (b, 0)),
            ] + [pl.BlockSpec(memory_space=pl.ANY)] * 9,
            out_specs=[
                pl.BlockSpec((count, 1, BLK), lambda b, s: (0, 0, 0)),
                pl.BlockSpec((blocks, 1, BLK), lambda b, s: (0, 0, 0)),
                pl.BlockSpec((2, width), lambda b, s: (0, 0)),
            ],
            scratch_shapes=[
                pltpu.VMEM((count, BLK, width), bf16),
                pltpu.VMEM((BLK, NBL * BLK), f32),
                pltpu.SemaphoreType.DMA((9,)),
            ],
        ),
        out_shape=[
            jax.ShapeDtypeStruct((count, 1, BLK), f32),
            jax.ShapeDtypeStruct((blocks, 1, BLK), f32),
            jax.ShapeDtypeStruct((2, width), f32),
        ],
        compiler_params=pltpu.CompilerParams(
            dimension_semantics=("arbitrary",), vmem_limit_bytes=40 * MIB
        ),
        cost_estimate=pl.CostEstimate(
            flops=8 * 10**9, bytes_accessed=20 * MIB, transcendentals=0
        ),
        name="softmax_grad",
    )(slots, dense, probe, *tables)


def weight_body(blocks, place, own_ref, twin_ref, far_ref, *rest):
    tables = rest[:9]
    out_ref, own, twin, far, table, total, sem = rest[9:]
    per = 3 * blocks
    copies = []
    for k in range(9):
        src, dst = ((own_ref, own), (twin_ref, twin), (far_ref, far))[k // 3]
        piece = pl.ds(k % 3 * blocks, blocks)
        copies.append((
            pltpu.make_async_copy(src.at[piece], dst.at[piece], sem.at[k]),
            pltpu.make_async_copy(tables[k], table.at[pl.ds(k * blocks, blocks)], sem.at[9 + k]),
        ))
    for pair in copies:
        for copy in pair:
            copy.start()
    for k in range(9):
        for copy in copies[k]:
            copy.wait()
        part = (own, twin, far)[k // 3]
        lhs = jnp.concatenate(
            [part[k % 3 * blocks + b].astype(bf16) for b in range(blocks)], axis=1
        )
        rhs = table[k * blocks:(k + 1) * blocks].reshape(blocks * BLK, table.shape[2])
        term = jnp.dot(lhs, rhs, preferred_element_type=f32)
        if k == 0:
            total[...] = term
        else:
            total[...] += term
    across = total.shape[1] // LANES
    for q in range(out_ref.shape[0]):
        r, c = q // across * 16, q % across * LANES
        out_ref[pl.ds(place[q], 1)] = total[r:r + 16, c:c + LANES][None]


def weight_terms(place, own, twin, far, tables):
    per, width, _ = own.shape
    depth = tables[0].shape[2]
    chunks = width * depth // (16 * LANES)
    return pl.pallas_call(
        functools.partial(weight_body, per // 3),
        grid_spec=pltpu.PrefetchScalarGridSpec(
            num_scalar_prefetch=1,
            grid=(1,),
            in_specs=[pl.BlockSpec(memory_space=pl.ANY)] * 12,
            out_specs=pl.BlockSpec((chunks, 16, LANES), lambda i, p: (0, 0, 0)),
            scratch_shapes=[
                pltpu.VMEM((per, width, BLK), f32),
                pltpu.VMEM((per, width, BLK), bf16),
                pltpu.VMEM((per, width, BLK), bf16),
                pltpu.VMEM((3 * per, BLK, depth), bf16),
                pltpu.VMEM((width, depth), f32),
                pltpu.SemaphoreType.DMA((18,)),
            ],
        ),
        out_shape=jax.ShapeDtypeStruct((chunks, 16, LANES), f32),
        compiler_params=pltpu.CompilerParams(
            dimension_semantics=("arbitrary",), vmem_limit_bytes=48 * MIB
        ),
        cost_estimate=pl.CostEstimate(
            flops=6 * 10**9, bytes_accessed=22 * MIB, transcendentals=0
        ),
        name="weight_terms",
    )(place, own, twin, far, *tables)


def finish_weight_body(scale, place, parts_ref, vec_ref, src_ref, dst_ref, out_ref, total):
    across = total.shape[1] // LANES
    for q in range(parts_ref.shape[0]):
        r, c = q // across * 16, q % across * LANES
        total[r:r + 16, c:c + LANES] = parts_ref[place[q]].astype(f32)
    full = total[...] + src_ref[...] * vec_ref[0:1, :] + dst_ref[...] * vec_ref[1:2, :]
    out_ref[...] = full.T * scale


def finish_weight(place, parts, vec, src, dst, scale):
    width, depth = src.shape[0], vec.shape[1]
    whole = lambda shape: pl.BlockSpec(shape, lambda i, p: (0,) * len(shape))
    return pl.pallas_call(
        functools.partial(finish_weight_body, scale),
        grid_spec=pltpu.PrefetchScalarGridSpec(
            num_scalar_prefetch=1,
            grid=(1,),
            in_specs=[whole(parts.shape), whole(vec.shape), whole(src.shape), whole(dst.shape)],
            out_specs=whole((depth, width)),
            scratch_shapes=[pltpu.VMEM((width, depth), f32)],
        ),
        out_shape=jax.ShapeDtypeStruct((depth, width), f32),
        compiler_params=pltpu.CompilerParams(
            dimension_semantics=("arbitrary",), vmem_limit_bytes=16 * MIB
        ),
        name="finish_weight",
    )(place, parts, vec, src, dst)


def finish_features_body(own_ref, twin_ref, far_ref, above_ref, below_ref, du_ref, sums_ref,
                         src_ref, dst_ref, weight_ref, out_ref):
    total = own_ref[0] + twin_ref[0].astype(f32) + far_ref[0].astype(f32)
    total = total + above_ref[0].astype(f32) + below_ref[0].astype(f32)
    total = total + src_ref[...] * du_ref[0] + dst_ref[...] * sums_ref[0]
    out_ref[...] = lax.dot_general(
        total.T.astype(bf16), weight_ref[...], (((1,), (1,)), ((), ())),
        preferred_element_type=f32,
    ).astype(bf16)


def finish_features(own, twin, far, above, below, du, sums, src, dst, weight):
    blocks, width, _ = above.shape
    depth = weight.shape[0]
    tile = pl.BlockSpec((1, width, BLK), lambda b: (b, 0, 0))
    line = pl.BlockSpec((1, 1, BLK), lambda b: (b, 0, 0))
    column = pl.BlockSpec((width, 1), lambda b: (0, 0))
    return pl.pallas_call(
        finish_features_body,
        grid=(blocks,),
        in_specs=[tile] * 5 + [line] * 2 + [column] * 2
        + [pl.BlockSpec(weight.shape, lambda b: (0, 0))],
        out_specs=pl.BlockSpec((BLK, depth), lambda b: (b, 0)),
        out_shape=jax.ShapeDtypeStruct((blocks * BLK, depth), bf16),
        compiler_params=pltpu.CompilerParams(
            dimension_semantics=("arbitrary",), vmem_limit_bytes=16 * MIB
        ),
        cost_estimate=pl.CostEstimate(
            flops=10**9, bytes_accessed=8 * MIB, transcendentals=0
        ),
        name="finish_features",
    )(own, twin, far, above, below, du, sums, src, dst, weight)


def ring(axis, low, count, offset):
    size = lax.axis_size(axis)
    turned = lambda i: ((i >> low) + offset) % count - (i >> low) % count
    return [(i, i + (turned(i) << low)) for i in range(size)]


def summed(parts, stages):
    tail = parts.shape[1:]
    parts = parts.reshape(tuple(n for _, _, n in stages) + tail)
    for axis, low, count in stages:
        total = parts[0]
        for k in range(1, count):
            total = total + lax.ppermute(parts[k], axis, ring(axis, low, count, k))
        parts = total
    for axis, low, count in stages[::-1]:
        parts = jnp.stack(
            [parts]
            + [lax.ppermute(parts, axis, ring(axis, low, count, k)) for k in range(1, count)]
        )
    return parts.reshape((-1,) + tail)


def summed_whole(array, stages):
    for axis, low, count in stages:
        others = [lax.ppermute(array, axis, ring(axis, low, count, k)) for k in range(1, count)]
        array = sum(others, array)
    return array


def places(stages, sign):
    chunk = jnp.arange(math.prod(n for _, _, n in stages), dtype=jnp.int32)
    place, stride = jnp.zeros_like(chunk), 1
    for axis, low, count in stages[::-1]:
        here = (lax.axis_index(axis) >> low) % count
        place = place + (sign * (chunk // stride % count - here)) % count * stride
        stride = stride * count
    return place


def on_device(features, weight, attn_src, attn_dst, upstream, scores, neighbour_lists, edge_index):
    rows, depth = features.shape
    width = weight.shape[1]
    blocks = rows // BLK
    size_x = lax.axis_size("gx")
    size_y = lax.axis_size("gy")
    here_x = lax.axis_index("gx")
    here_y = lax.axis_index("gy")
    twin = [(i, i ^ 1) for i in range(size_x)]
    far = [(i, (((i + 1) ^ 1) - 1) % size_x) for i in range(size_x)]
    up = [(i, (i + 1) % size_y) for i in range(size_y)]
    down = [(i, (i - 1) % size_y) for i in range(size_y)]

    owner = neighbour_lists // blocks
    owner_x, owner_y = owner // size_y, owner % size_y
    part_x = jnp.where(owner_x == here_x, 0, jnp.where(owner_x // 2 == here_x // 2, 1, 2))
    part_y = jnp.where(owner_y == here_y, 0, jnp.where(owner_y == (here_y + 1) % size_y, 1, 2))
    slots = (part_x * 3 + part_y) * blocks + neighbour_lists % blocks

    own = features.reshape(blocks, BLK, depth)
    above = lax.ppermute(own, "gy", down)
    below = lax.ppermute(own, "gy", up)
    tables = [own, above, below]
    tables = tables + [lax.ppermute(t, "gx", twin) for t in tables] + [
        lax.ppermute(t, "gx", far) for t in tables
    ]

    dense, acc_own, acc_twin, acc_far = spread(slots, scores, edge_index, upstream)
    probe = lax.dot_general(
        upstream, weight, (((1,), (1,)), ((), ())), preferred_element_type=f32
    ).astype(bf16)

    stages = (("gx", 0, 2), ("gx", 1, size_x // 2), ("gy", 0, 4), ("gy", 2, size_y // 4))
    terms = weight_terms(places(stages, 1), acc_own, acc_twin, acc_far, tables)
    weight_total = summed(terms, stages)

    split = (3, blocks, width, BLK)
    acc_own = acc_own.reshape(split)
    from_twin = lax.ppermute(acc_twin, "gx", twin).reshape(split)
    from_far = lax.ppermute(acc_far, "gx", far).reshape(split)
    column = [
        (acc_own[k] + from_twin[k].astype(f32) + from_far[k].astype(f32)).astype(bf16)
        for k in (1, 2)
    ]
    from_below = lax.ppermute(column[0], "gy", up)
    from_above = lax.ppermute(column[1], "gy", down)

    sums, du, vec = softmax_grad(slots, dense, probe, tables)
    sums = sums.reshape(3, 3, blocks, 1, BLK)
    sums = sums[0] + lax.ppermute(sums[1], "gx", twin) + lax.ppermute(sums[2], "gx", far)
    sums = sums[0] + lax.ppermute(sums[1], "gy", up) + lax.ppermute(sums[2], "gy", down)

    src = attn_src[:, None]
    dst = attn_dst[:, None]
    grad_features = finish_features(
        acc_own[0], from_twin[0], from_far[0], from_above, from_below, du, sums, src, dst, weight
    )

    scale = 1.0 / math.sqrt(rows * size_x * size_y)
    vec = summed_whole(vec, stages)
    vectors = jnp.dot(vec, weight.astype(f32), precision=lax.Precision.HIGHEST) * scale
    grad_weight = finish_weight(places(stages, -1), weight_total, vec, src, dst, scale)
    return (grad_features, grad_weight, vectors[0], vectors[1])


def solution(mesh):
    rows = P(("gx", "gy"), None)
    return jax.shard_map(
        on_device,
        mesh=mesh,
        in_specs=(rows, P(), P(), P(), rows, rows, rows, rows),
        out_specs=(rows, P(), P(), P()),
        check_vma=False,
    )
```

```python
import functools
import math

import jax
import jax.numpy as jnp
from jax import lax
from jax.experimental import pallas as pl
from jax.experimental.pallas import tpu as pltpu
from jax.sharding import PartitionSpec as P

BLK = 128
NBL = 16
WIDE = 256
HALVES = NBL * BLK // WIDE
LANES = 128
CHUNK = 64
MIB = 1 << 20

f32 = jnp.float32
bf16 = jnp.bfloat16


def spread_body(edges, slots, score_ref, index_ref, grad_ref, dense_ref, twin_ref, far_a_ref,
                far_b_ref, left_scr, right_scr, grad_t, acc):
    step = pl.program_id(0)

    @pl.when(step == 0)
    def _():
        acc[...] = jnp.zeros_like(acc)

    grad_t[...] = grad_ref[...].T
    pad = ((0, LANES - edges), (0, 0))
    score = score_ref[...]
    logit = jnp.where(score > 0, score, 0.2 * score)
    expo = jnp.exp(logit - jnp.max(logit, axis=0, keepdims=True))
    alpha = expo / jnp.sum(expo, axis=0, keepdims=True)
    main = alpha.astype(bf16).astype(f32)
    rest = (alpha - main).astype(bf16).astype(f32)
    index = index_ref[...]
    low = (index % WIDE).astype(f32)
    high = jnp.pad((index // WIDE).astype(f32), pad, constant_values=-1.0).T
    main = jnp.pad(jnp.where(score > 0, main, -main), pad).T
    rest = jnp.pad(jnp.where(score > 0, rest, -rest), pad).T

    lanes = lax.broadcasted_iota(jnp.int32, (edges, LANES), 1).astype(f32).astype(bf16)
    halves = lax.broadcasted_iota(jnp.int32, (HALVES, LANES), 0).astype(f32)
    one = jnp.ones((edges, LANES), bf16)
    none = jnp.zeros((edges, LANES), bf16)
    tail = jnp.zeros((LANES - edges, WIDE), bf16)
    for i in range(BLK):
        here = jnp.broadcast_to(high[i:i + 1, :], (HALVES, LANES)) == halves
        lhs = jnp.concatenate(
            [
                jnp.where(here, jnp.broadcast_to(term[i:i + 1, :], (HALVES, LANES)), 0.0)
                for term in (main, rest)
            ],
            axis=0,
        ).astype(bf16)
        column = jnp.broadcast_to(low[:, i:i + 1], (edges, LANES)).astype(bf16)
        rhs = jnp.concatenate(
            [jnp.where(column == lanes + LANES * c, one, none) for c in range(WIDE // LANES)],
            axis=1,
        )
        rhs = jnp.concatenate([rhs, tail], axis=0)
        out = jnp.dot(lhs, rhs, preferred_element_type=f32)
        left_scr[2 * HALVES * i:2 * HALVES * (i + 1), :] = out[:, :LANES]
        right_scr[2 * HALVES * i:2 * HALVES * (i + 1), :] = out[:, LANES:]
    for s in range(NBL):
        scr = (left_scr, right_scr)[s % 2]
        main = scr[pl.ds(s // 2, BLK, stride=2 * HALVES), :]
        rest = scr[pl.ds(HALVES + s // 2, BLK, stride=2 * HALVES), :]
        dense_ref[0, :, s * BLK:(s + 1) * BLK] = main + rest
        low = jnp.abs(main).astype(bf16)
        acc[pl.ds(slots[step, s], 1)] += jnp.dot(grad_t[...], low, preferred_element_type=f32)[None]

    @pl.when(step == pl.num_programs(0) - 1)
    def _():
        per, width, _ = twin_ref.shape
        half = width // 2

        def cast(k, carry):
            twin_ref[pl.ds(k, 1)] = acc[pl.ds(k, 1)].astype(bf16)
            far_a_ref[pl.ds(k, 1)] = acc[pl.ds(per + k, 1), :half].astype(bf16)
            far_b_ref[pl.ds(k, 1)] = acc[pl.ds(per + k, 1), half:].astype(bf16)
            return carry

        lax.fori_loop(0, per, cast, 0)


def spread(slots, scores, index, grad):
    edges, rows = scores.shape
    blocks = rows // BLK
    width = grad.shape[1]
    per = 3 * blocks
    sent = [(per, width, BLK), (per, width // 2, BLK), (per, width // 2, BLK)]
    return pl.pallas_call(
        functools.partial(spread_body, edges),
        grid_spec=pltpu.PrefetchScalarGridSpec(
            num_scalar_prefetch=1,
            grid=(blocks,),
            in_specs=[pl.BlockSpec((edges, BLK), lambda b, s: (0, b))] * 2
            + [pl.BlockSpec((BLK, width), lambda b, s: (b, 0))],
            out_specs=[pl.BlockSpec((1, BLK, NBL * BLK), lambda b, s: (b, 0, 0))] + [
                pl.BlockSpec(shape, lambda b, s: (0, 0, 0), pipeline_mode=pl.Buffered(1))
                for shape in sent
            ],
            scratch_shapes=[
                pltpu.VMEM((2 * HALVES * BLK, LANES), f32),
                pltpu.VMEM((2 * HALVES * BLK, LANES), f32),
                pltpu.VMEM((width, BLK), bf16),
                pltpu.VMEM((2 * per + 1, width, BLK), f32),
            ],
        ),
        out_shape=[jax.ShapeDtypeStruct((blocks, BLK, NBL * BLK), f32)]
        + [jax.ShapeDtypeStruct(shape, bf16) for shape in sent],
        compiler_params=pltpu.CompilerParams(
            dimension_semantics=("arbitrary",), vmem_limit_bytes=60 * MIB
        ),
        cost_estimate=pl.CostEstimate(
            flops=24 * 10**9, bytes_accessed=MIB, transcendentals=0
        ),
        name="spread",
    )(jnp.where(slots >= per, slots - per, 2 * per), scores, index, grad)


def collect_body(slots, dense_ref, grad_ref, own_ref, grad_t, acc):
    step = pl.program_id(0)

    @pl.when(step == 0)
    def _():
        acc[...] = jnp.zeros_like(acc)

    grad_t[...] = grad_ref[...].T
    for s in range(NBL):
        low = jnp.abs(dense_ref[0, :, s * BLK:(s + 1) * BLK]).astype(bf16)
        acc[pl.ds(slots[step, s], 1)] += jnp.dot(grad_t[...], low, preferred_element_type=f32)[None]

    @pl.when(step == pl.num_programs(0) - 1)
    def _():
        own_ref[...] = acc[:own_ref.shape[0]]


def collect(slots, dense, grad):
    blocks = dense.shape[0]
    width = grad.shape[1]
    per = 3 * blocks
    return pl.pallas_call(
        collect_body,
        grid_spec=pltpu.PrefetchScalarGridSpec(
            num_scalar_prefetch=1,
            grid=(blocks,),
            in_specs=[
                pl.BlockSpec((1, BLK, NBL * BLK), lambda b, s: (b, 0, 0)),
                pl.BlockSpec((BLK, width), lambda b, s: (b, 0)),
            ],
            out_specs=pl.BlockSpec(
                (per, width, BLK), lambda b, s: (0, 0, 0), pipeline_mode=pl.Buffered(1)
            ),
            scratch_shapes=[
                pltpu.VMEM((width, BLK), bf16),
                pltpu.VMEM((per + 1, width, BLK), f32),
            ],
        ),
        out_shape=jax.ShapeDtypeStruct((per, width, BLK), f32),
        compiler_params=pltpu.CompilerParams(
            dimension_semantics=("arbitrary",), vmem_limit_bytes=48 * MIB
        ),
        cost_estimate=pl.CostEstimate(
            flops=11 * 10**9, bytes_accessed=MIB, transcendentals=0
        ),
        name="collect",
    )(jnp.minimum(slots, per), dense, grad)


def two_terms(row, first, rows):
    at = lax.broadcasted_iota(jnp.int32, (rows, row.shape[1]), 0)
    row = jnp.broadcast_to(row, at.shape)
    main = row.astype(bf16).astype(f32)
    return jnp.where(at == first, main, jnp.where(at == first + 1, row - main, 0.0))


def gradients_body(blocks, pieces, place, slots, dense_ref, probe_ref, grad_ref, *rest):
    count = len(pieces)
    tables = rest[:count]
    sums_ref, du_ref, keep_ref, send_ref = rest[count:count + 4]
    table, prod, mixed, grad_t, vec, total, sem = rest[count + 4:]
    step = pl.program_id(0)
    depth = table.shape[2]

    @pl.when(step == 0)
    def _():
        copies = [
            pltpu.make_async_copy(t, table.at[pl.ds(first, size)], sem.at[k])
            for k, (t, (first, size)) in enumerate(zip(tables, pieces))
        ]
        for copy in copies:
            copy.start()
        sums_ref[...] = jnp.zeros_like(sums_ref)
        vec[...] = jnp.zeros_like(vec)
        for copy in copies:
            copy.wait()

    inner = jnp.zeros((BLK, BLK), f32)
    sized = jnp.zeros((BLK, BLK), f32)
    for s in range(NBL):
        cols = slice(s * BLK, (s + 1) * BLK)
        cand = table[slots[step, s]]
        d = lax.dot_general(
            probe_ref[...], cand, (((1,), (1,)), ((), ())), preferred_element_type=f32
        )
        prod[:, cols] = d
        a = jnp.abs(dense_ref[0, :, cols])
        inner = inner + a * d
        sized = sized + a
    mean = jnp.sum(inner, axis=1, keepdims=True) / jnp.sum(sized, axis=1, keepdims=True)
    du = jnp.zeros((BLK, BLK), f32)
    mix = jnp.zeros((BLK + 16, depth), f32)
    for s in range(NBL):
        cols = slice(s * BLK, (s + 1) * BLK)
        a = dense_ref[0, :, cols]
        dz = jnp.where(a > 0, a, -0.2 * a) * (prod[:, cols] - mean)
        du = du + dz
        slot = slots[step, s]
        sums = jnp.sum(dz, axis=0, keepdims=True)
        sums_ref[pl.ds(slot, 1)] += sums[None]
        lhs = jnp.concatenate(
            [jnp.abs(a).astype(bf16), two_terms(sums, 0, 16).astype(bf16)], axis=0
        )
        mix = mix + jnp.dot(lhs, table[slot], preferred_element_type=f32)
    row = jnp.broadcast_to(jnp.sum(du, axis=1, keepdims=True), (BLK, BLK)).T[0:1, :]
    du_ref[pl.ds(step, 1)] = row[None]
    mixed[step] = mix[:BLK].astype(bf16)
    vec[...] += mix[BLK:] + jnp.dot(
        two_terms(row, 2, 16).astype(bf16), table[step], preferred_element_type=f32
    )
    grad_t[step] = grad_ref[...].T

    @pl.when(step == pl.num_programs(0) - 1)
    def _():
        lhs = jnp.concatenate([grad_t[b] for b in range(blocks)], axis=1)
        rhs = mixed[...].reshape(blocks * BLK, depth)
        total[...] = jnp.dot(lhs, rhs, preferred_element_type=f32)
        across = depth // LANES
        chunks = keep_ref.shape[0] // CHUNK
        for q in range(2 * chunks):
            r, c = q // across * CHUNK, q % across * LANES
            p = place[q]
            tile = total[r:r + CHUNK, c:c + LANES]

            @pl.when(p < chunks)
            def _():
                keep_ref[pl.ds(pl.multiple_of(p * CHUNK, CHUNK), CHUNK), :] = tile

            @pl.when(p >= chunks)
            def _():
                send_ref[pl.ds(pl.multiple_of((p - chunks) * CHUNK, CHUNK), CHUNK), :] = tile

        ends = jnp.concatenate(
            [
                (vec[r:r + 1, :] + vec[r + 1:r + 2, :])[:, c * LANES:(c + 1) * LANES]
                for r in (2, 0)
                for c in range(across)
            ],
            axis=0,
        )
        keep_ref[chunks * CHUNK:, :] = ends
        send_ref[chunks * CHUNK:, :] = ends


def gradients(place, slots, dense, probe, grad, pieces, tables):
    blocks = dense.shape[0]
    width = grad.shape[1]
    depth = probe.shape[1]
    count = 9 * blocks
    message = (width * depth // (2 * LANES) + 8, LANES)
    fixed = lambda shape: pl.BlockSpec(shape, lambda b, p, s: (0,) * len(shape))
    return pl.pallas_call(
        functools.partial(gradients_body, blocks, pieces),
        grid_spec=pltpu.PrefetchScalarGridSpec(
            num_scalar_prefetch=2,
            grid=(blocks,),
            in_specs=[
                pl.BlockSpec((1, BLK, NBL * BLK), lambda b, p, s: (b, 0, 0)),
                pl.BlockSpec((BLK, depth), lambda b, p, s: (b, 0)),
                pl.BlockSpec((BLK, width), lambda b, p, s: (b, 0)),
            ] + [pl.BlockSpec(memory_space=pl.ANY)] * len(tables),
            out_specs=[
                fixed((count, 1, BLK)), fixed((blocks, 1, BLK)), fixed(message), fixed(message)
            ],
            scratch_shapes=[
                pltpu.VMEM((count, BLK, depth), bf16),
                pltpu.VMEM((BLK, NBL * BLK), f32),
                pltpu.VMEM((blocks, BLK, depth), bf16),
                pltpu.VMEM((blocks, width, BLK), bf16),
                pltpu.VMEM((16, depth), f32),
                pltpu.VMEM((width, depth), f32),
                pltpu.SemaphoreType.DMA((len(tables),)),
            ],
        ),
        out_shape=[
            jax.ShapeDtypeStruct((count, 1, BLK), f32),
            jax.ShapeDtypeStruct((blocks, 1, BLK), f32),
            jax.ShapeDtypeStruct(message, f32),
            jax.ShapeDtypeStruct(message, f32),
        ],
        compiler_params=pltpu.CompilerParams(
            dimension_semantics=("arbitrary",), vmem_limit_bytes=60 * MIB
        ),
        cost_estimate=pl.CostEstimate(flops=22 * 10**9, bytes_accessed=MIB, transcendentals=0),
        name="gradients",
    )(place, slots, dense, probe, grad, *tables)


def columns_of(row):
    return jnp.broadcast_to(row, (LANES, row.shape[1])).T


def finish_weight_body(scale, place, near_ref, away_ref, vec_ref, src_ref, dst_ref, weight_ref,
                       out_ref, grad_src_ref, grad_dst_ref, total):
    across = total.shape[1] // LANES
    chunks = near_ref.shape[0]
    for q in range(2 * chunks):
        r, c = q // across * CHUNK, q % across * LANES
        p = place[q]
        at = lax.rem(p, chunks)
        tile = jnp.where(p < chunks, near_ref[at].astype(f32), away_ref[at].astype(f32))
        total[r:r + CHUNK, c:c + LANES] = tile
    rows = [
        jnp.concatenate([vec_ref[v * across + c][None] for c in range(across)], axis=1)
        for v in range(2)
    ]
    full = total[...]
    for ref, row in zip((src_ref, dst_ref), rows):
        full = full + jnp.concatenate([columns_of(ref[...])] * across, axis=1) * row
    out_ref[...] = full.T * scale
    terms = [two_terms(rows[0], 0, 16), two_terms(rows[1], 2, 16)]
    for v, row in enumerate(rows):
        main = row.astype(bf16).astype(f32)
        last = row - main
        last = last - last.astype(bf16).astype(f32)
        at = lax.broadcasted_iota(jnp.int32, (16, row.shape[1]), 0)
        terms.append(jnp.where(at == 4 + v, last, 0.0))
    lhs = sum(terms[1:], terms[0]).astype(bf16)
    out = jnp.dot(lhs, weight_ref[...], preferred_element_type=f32) * scale
    grad_src_ref[...] = (out[0:1, :] + out[1:2, :] + out[4:5, :]).reshape(out.shape[1])
    grad_dst_ref[...] = (out[2:3, :] + out[3:4, :] + out[5:6, :]).reshape(out.shape[1])


def finish_weight(place, near, away, vec, src, dst, weight, scale):
    depth, width = weight.shape
    whole = lambda shape: pl.BlockSpec(shape, lambda i, p: (0,) * len(shape))
    args = (near, away, vec, src, dst, weight)
    return pl.pallas_call(
        functools.partial(finish_weight_body, scale),
        grid_spec=pltpu.PrefetchScalarGridSpec(
            num_scalar_prefetch=1,
            grid=(1,),
            in_specs=[whole(a.shape) for a in args],
            out_specs=[whole((depth, width)), whole((width,)), whole((width,))],
            scratch_shapes=[pltpu.VMEM((width, depth), f32)],
        ),
        out_shape=[
            jax.ShapeDtypeStruct((depth, width), f32),
            jax.ShapeDtypeStruct((width,), f32),
            jax.ShapeDtypeStruct((width,), f32),
        ],
        compiler_params=pltpu.CompilerParams(
            dimension_semantics=("arbitrary",), vmem_limit_bytes=60 * MIB
        ),
        name="finish_weight",
    )(place, *args)


def finish_features_body(own_ref, twin_ref, far_a_ref, far_b_ref, above_a_ref, above_b_ref,
                         below_a_ref, below_b_ref, du_ref, sums_ref, src_ref, dst_ref, weight_ref,
                         out_ref, src_cols, dst_cols):
    @pl.when(pl.program_id(0) == 0)
    def _():
        src_cols[...] = columns_of(src_ref[...])
        dst_cols[...] = columns_of(dst_ref[...])

    half = far_a_ref.shape[1]
    both = lambda a, b: jnp.concatenate(
        [a[0].astype(f32), b[0, :half].astype(f32)], axis=0
    )
    total = own_ref[0] + twin_ref[0].astype(f32) + both(far_a_ref, far_b_ref)
    total = total + both(above_a_ref, above_b_ref) + both(below_a_ref, below_b_ref)
    sums = sums_ref[0]
    for ref in (above_b_ref, below_b_ref):
        carried = ref[0, half:half + 16].astype(f32)
        sums = sums + carried[0:1] + carried[1:2] + carried[2:3]
    total = total + src_cols[...] * du_ref[0] + dst_cols[...] * sums
    out_ref[...] = lax.dot_general(
        total.T.astype(bf16), weight_ref[...], (((1,), (1,)), ((), ())),
        preferred_element_type=f32,
    ).astype(bf16)


def finish_features(own, twin, halves, du, sums, src, dst, weight):
    blocks = du.shape[0]
    depth, width = weight.shape
    tile = lambda array: pl.BlockSpec((1,) + array.shape[1:], lambda b: (b, 0, 0))
    line = pl.BlockSpec((1, width), lambda b: (0, 0))
    arrays = [own, twin, *halves, du, sums]
    return pl.pallas_call(
        finish_features_body,
        grid=(blocks,),
        in_specs=[tile(array) for array in arrays] + [line] * 2
        + [pl.BlockSpec(weight.shape, lambda b: (0, 0))],
        out_specs=pl.BlockSpec((BLK, depth), lambda b: (b, 0)),
        scratch_shapes=[pltpu.VMEM((width, BLK), f32)] * 2,
        out_shape=jax.ShapeDtypeStruct((blocks * BLK, depth), bf16),
        compiler_params=pltpu.CompilerParams(
            dimension_semantics=("arbitrary",), vmem_limit_bytes=60 * MIB
        ),
        cost_estimate=pl.CostEstimate(
            flops=9 * 10**9, bytes_accessed=MIB, transcendentals=0
        ),
        name="finish_features",
    )(*arrays, src, dst, weight)


def ring(axis, low, count, offset):
    size = lax.axis_size(axis)
    turned = lambda i: ((i >> low) + offset) % count - (i >> low) % count
    return [(i, i + (turned(i) << low)) for i in range(size)]


def turned(array, stage):
    axis, low, count = stage
    return [lax.ppermute(array, axis, ring(axis, low, count, k)) for k in range(1, count)]


def scattered(array, stage, tail):
    axis, low, count = stage
    rows = (array.shape[0] - tail) // count
    chunk = lambda k: jnp.concatenate([array[k * rows:(k + 1) * rows], array[count * rows:]])
    total = chunk(0)
    for k in range(1, count):
        total = total + lax.ppermute(chunk(k), axis, ring(axis, low, count, k))
    return total


def after(array, *others):
    return lax.optimization_barrier((array, *others))[0]


def places(stages, sign):
    chunk = jnp.arange(math.prod(n for _, _, n in stages), dtype=jnp.int32)
    place, stride = jnp.zeros_like(chunk), 1
    for axis, low, count in stages[::-1]:
        here = (lax.axis_index(axis) >> low) % count
        place = place + (sign * (chunk // stride % count - here)) % count * stride
        stride = stride * count
    return place


def on_device(features, weight, attn_src, attn_dst, upstream, scores, neighbour_lists, edge_index):
    rows, depth = features.shape
    width = weight.shape[1]
    blocks = rows // BLK
    size_x = lax.axis_size("gx")
    size_y = lax.axis_size("gy")
    here_x = lax.axis_index("gx")
    here_y = lax.axis_index("gy")
    twin = [(i, i ^ 1) for i in range(size_x)]
    far = [(i, (((i + 1) ^ 1) - 1) % size_x) for i in range(size_x)]
    up = [(i, (i + 1) % size_y) for i in range(size_y)]
    down = [(i, (i - 1) % size_y) for i in range(size_y)]

    owner = neighbour_lists // blocks
    owner_x, owner_y = owner // size_y, owner % size_y
    part_x = jnp.where(owner_x == here_x, 0, jnp.where(owner_x // 2 == here_x // 2, 1, 2))
    part_y = jnp.where(owner_y == here_y, 0, jnp.where(owner_y == (here_y + 1) % size_y, 1, 2))
    slots = (part_x * 3 + part_y) * blocks + neighbour_lists % blocks

    own = features.reshape(blocks, BLK, depth)
    above = lax.ppermute(own, "gy", down)
    below = lax.ppermute(own, "gy", up)
    away = lax.ppermute(own, "gx", far)
    across = lax.ppermute(own, "gx", twin)
    dense, acc_twin, acc_far_a, acc_far_b = spread(slots, scores.T, edge_index.T, upstream)
    (above, below, away, across, dense, acc_twin, acc_far_a, acc_far_b) = (
        lax.optimization_barrier(
            (above, below, away, across, dense, acc_twin, acc_far_a, acc_far_b)
        )
    )
    from_y = [lax.ppermute(away, "gy", down), lax.ppermute(away, "gy", up)]
    from_far = [lax.ppermute(acc_far_a, "gx", far)]
    from_twin = lax.ppermute(acc_twin, "gx", twin)
    sides = lax.ppermute(jnp.concatenate([above, below]), "gx", twin)
    probe = lax.dot_general(
        upstream, weight, (((1,), (1,)), ((), ())), preferred_element_type=f32
    ).astype(bf16)
    acc_own = collect(slots, after(dense, probe), upstream)
    acc_own, from_twin, from_far[0] = lax.optimization_barrier((acc_own, from_twin, from_far[0]))

    def column(k, h, far_half):
        rows = slice(k * blocks, (k + 1) * blocks)
        cols = slice(h * width // 2, (h + 1) * width // 2)
        total = acc_own[rows, cols] + from_twin[rows, cols].astype(f32)
        return total + far_half[rows].astype(f32)

    to_above = column(1, 0, from_far[0]).astype(bf16)
    to_below = column(2, 0, from_far[0]).astype(bf16)
    dense, to_above, to_below, acc_far_b, sides, *from_y = lax.optimization_barrier(
        (dense, to_above, to_below, acc_far_b, sides, *from_y)
    )
    from_far.append(lax.ppermute(acc_far_b, "gx", far))
    from_below = [lax.ppermute(to_above, "gy", up)]
    from_above = [lax.ppermute(to_below, "gy", down)]
    tables = [own, above, below, across, sides, away, *from_y]
    firsts = (0, 1, 2, 3, 4, 6, 7, 8)
    pieces = tuple((k * blocks, t.shape[0]) for k, t in zip(firsts, tables))

    core, along_x, along_z = ("gx", 0, 2), ("gy", 2, size_y // 4), ("gx", 1, size_x // 2)
    stages = (core, along_x, along_z)
    sums, du, keep, send = gradients(
        places(stages, 1), slots, dense, probe, upstream, pieces, tables
    )
    sums, du, keep, send, from_below[0], from_above[0] = lax.optimization_barrier(
        (sums, du, keep, send, from_below[0], from_above[0])
    )
    sums = sums.reshape(3, 3, blocks, 1, BLK)
    part = keep + lax.ppermute(send, "gx", twin)
    sums = sums[0] + lax.ppermute(sums[1], "gx", twin) + lax.ppermute(sums[2], "gx", far)
    part, sums, far_b = lax.optimization_barrier((part, sums, from_far[1]))

    def terms(row):
        main = row.astype(bf16)
        rest = row - main.astype(f32)
        next_ = rest.astype(bf16)
        last = (rest - next_.astype(f32)).astype(bf16)
        pad = jnp.zeros((blocks, 13, BLK), bf16)
        return jnp.concatenate([main, next_, last, pad], axis=1)

    to_above = jnp.concatenate([column(1, 1, far_b).astype(bf16), terms(sums[1])], axis=1)
    to_below = jnp.concatenate([column(2, 1, far_b).astype(bf16), terms(sums[2])], axis=1)
    part, to_above, to_below = lax.optimization_barrier((part, to_above, to_below))
    from_below.append(lax.ppermute(to_above, "gy", up))
    from_above.append(lax.ppermute(to_below, "gy", down))
    part = scattered(part, along_x, 8)
    part = scattered(part, along_z, 8)
    part, from_below[1], from_above[1] = lax.optimization_barrier(
        (part, from_below[1], from_above[1])
    )
    part = sum(turned(part, ("gy", 0, 4)), part)
    vec = part[CHUNK:]
    part = part[:CHUNK].astype(bf16)
    part = jnp.stack([part] + turned(part, along_z))
    part, du = lax.optimization_barrier((part, du))
    part = jnp.concatenate([part] + turned(part, along_x))
    src, dst = attn_src[None], attn_dst[None]
    grad_features = finish_features(
        acc_own, from_twin, [from_far[0], far_b] + from_above + from_below, du, sums[0], src, dst,
        weight
    )
    part, grad_features = lax.optimization_barrier((part, grad_features))
    scale = 1.0 / math.sqrt(rows * size_x * size_y)
    grad_weight, grad_src, grad_dst = finish_weight(
        places(stages, -1), part, lax.ppermute(part, "gx", twin), vec, src, dst, weight, scale
    )
    return (grad_features, grad_weight, grad_src, grad_dst)


def solution(mesh):
    rows = P(("gx", "gy"), None)
    return jax.shard_map(
        on_device,
        mesh=mesh,
        in_specs=(rows, P(), P(), P(), rows, rows, rows, rows),
        out_specs=(rows, P(), P(), P()),
        check_vma=False,
    )
```

```python
import functools
import math

import jax
import jax.numpy as jnp
from jax import lax
from jax.experimental import pallas as pl
from jax.experimental.pallas import tpu as pltpu
from jax.sharding import PartitionSpec as P

BLK = 128
NBL = 16
WIDE = 256
HALVES = NBL * BLK // WIDE
LANES = 128
CHUNK = 64
JOINED = 4
MIB = 1 << 20

f32 = jnp.float32
bf16 = jnp.bfloat16


def spread_body(edges, slots, score_ref, index_ref, grad_ref, dense_ref, own_ref, twin_o_ref,
                twin_ref, far_o_ref, far_ref, grad_t, left_scr, right_scr, low_scr, high_scr, main_scr, rest_scr, dense,
                acc, sem):
    blocks = dense.shape[0]
    pad = ((0, LANES - edges), (0, 0))
    lanes = lax.broadcasted_iota(jnp.int32, (edges, LANES), 1).astype(f32).astype(bf16)
    halves = lax.broadcasted_iota(jnp.int32, (HALVES, LANES), 0).astype(f32)
    one = jnp.ones((edges, LANES), bf16)
    none = jnp.zeros((edges, LANES), bf16)
    tail = jnp.zeros((LANES - edges, WIDE), bf16)
    acc[...] = jnp.zeros_like(acc)
    score = score_ref[...]
    logit = jnp.where(score > 0, score, 0.2 * score)
    expo = jnp.exp(logit - jnp.max(logit, axis=0, keepdims=True))
    alpha = expo / jnp.sum(expo, axis=0, keepdims=True)
    main = alpha.astype(bf16).astype(f32)
    rest = (alpha - main).astype(bf16).astype(f32)
    index = index_ref[...]
    low_scr[...] = (index % WIDE).astype(f32)
    high = jnp.pad((index // WIDE).astype(f32), pad, constant_values=-1.0)
    main = jnp.pad(jnp.where(score > 0, main, -main), pad)
    rest = jnp.pad(jnp.where(score > 0, rest, -rest), pad)
    for b in range(blocks):
        nodes = slice(b * BLK, (b + 1) * BLK)
        high_scr[nodes, :] = high[:, nodes].T
        main_scr[nodes, :] = main[:, nodes].T
        rest_scr[nodes, :] = rest[:, nodes].T
        grad_t[b] = grad_ref[nodes, :].T

    def out_copy(step):
        return pltpu.make_async_copy(dense.at[step], dense_ref.at[step], sem.at[step])

    def block(step, carry):
        nodes = pl.ds(pl.multiple_of(step * BLK, BLK), BLK)
        low = low_scr[:, nodes]
        high, main, rest = high_scr[nodes, :], main_scr[nodes, :], rest_scr[nodes, :]
        for i in range(BLK):
            here = jnp.broadcast_to(high[i:i + 1, :], (HALVES, LANES)) == halves
            lhs = jnp.concatenate(
                [
                    jnp.where(here, jnp.broadcast_to(term[i:i + 1, :], (HALVES, LANES)), 0.0)
                    for term in (main, rest)
                ],
                axis=0,
            ).astype(bf16)
            column = jnp.broadcast_to(low[:, i:i + 1], (edges, LANES)).astype(bf16)
            rhs = jnp.concatenate(
                [jnp.where(column == lanes + LANES * c, one, none) for c in range(WIDE // LANES)],
                axis=1,
            )
            rhs = jnp.concatenate([rhs, tail], axis=0)
            out = jnp.dot(lhs, rhs, preferred_element_type=f32)
            left_scr[2 * HALVES * i:2 * HALVES * (i + 1), :] = out[:, :LANES]
            right_scr[2 * HALVES * i:2 * HALVES * (i + 1), :] = out[:, LANES:]
        for s in range(NBL):
            scr = (left_scr, right_scr)[s % 2]
            main = scr[pl.ds(s // 2, BLK, stride=2 * HALVES), :]
            rest = scr[pl.ds(HALVES + s // 2, BLK, stride=2 * HALVES), :]
            dense[step, :, s * BLK:(s + 1) * BLK] = main + rest
            low = jnp.abs(main).astype(bf16)
            term = jnp.dot(grad_t[step], low, preferred_element_type=f32)[None]
            acc[pl.ds(slots[step, s], 1)] += term
        out_copy(step).start()
        return carry

    lax.fori_loop(0, blocks, block, 0)
    per = own_ref.shape[0]

    def cast(k, carry):
        own_ref[pl.ds(k, 1)] = acc[pl.ds(2 * per + k, 1)]
        return carry

    def cast_own(k, carry):
        twin_o_ref[pl.ds(k, 1)] = acc[pl.ds(k, 1)].astype(bf16)
        far_o_ref[pl.ds(k, 1)] = acc[pl.ds(per + k, 1)].astype(bf16)
        return carry

    def cast_sides(k, carry):
        twin_ref[pl.ds(k, 1)] = acc[pl.ds(blocks + k, 1)].astype(bf16)
        far_ref[pl.ds(k, 1)] = acc[pl.ds(per + blocks + k, 1)].astype(bf16)
        return carry

    lax.fori_loop(0, per, cast, 0)
    lax.fori_loop(0, blocks, cast_own, 0)
    lax.fori_loop(0, per - blocks, cast_sides, 0)
    lax.fori_loop(0, blocks, lambda step, carry: (out_copy(step).wait(), carry)[1], 0)


def fixed(shape):
    return pl.BlockSpec(shape, lambda *_: (0,) * len(shape), pipeline_mode=pl.Buffered(1))


def spread(slots, scores, index, grad):
    edges, rows = scores.shape
    blocks = rows // BLK
    width = grad.shape[1]
    per = 3 * blocks
    away = [(blocks, width, BLK), (2 * blocks, width, BLK)]
    sums = [(per, width, BLK)] + away + away + [(blocks, width, BLK)]
    types = [f32] + [bf16] * 5
    dense = (blocks, BLK, NBL * BLK)
    return pl.pallas_call(
        functools.partial(spread_body, edges),
        grid_spec=pltpu.PrefetchScalarGridSpec(
            num_scalar_prefetch=1,
            grid=(1,),
            in_specs=[fixed(scores.shape), fixed(index.shape), fixed(grad.shape)],
            out_specs=[pl.BlockSpec(memory_space=pl.ANY)] + [fixed(shape) for shape in sums],
            scratch_shapes=[
                pltpu.VMEM((2 * HALVES * BLK, LANES), f32),
                pltpu.VMEM((2 * HALVES * BLK, LANES), f32),
                pltpu.VMEM((edges, rows), f32),
                pltpu.VMEM((rows, LANES), f32),
                pltpu.VMEM((rows, LANES), f32),
                pltpu.VMEM((rows, LANES), f32),
                pltpu.VMEM(dense, f32),
                pltpu.VMEM((3 * per, width, BLK), f32),
                pltpu.SemaphoreType.DMA((blocks,)),
            ],
        ),
        out_shape=[jax.ShapeDtypeStruct(dense, f32)]
        + [jax.ShapeDtypeStruct(*pair) for pair in zip(sums, types)],
        compiler_params=pltpu.CompilerParams(
            dimension_semantics=("arbitrary",), vmem_limit_bytes=60 * MIB
        ),
        cost_estimate=pl.CostEstimate(flops=0, bytes_accessed=0, transcendentals=0),
        name="spread",
    )((slots + 2 * per) % (3 * per), scores, index, grad)


def two_terms(row, first, rows):
    at = lax.broadcasted_iota(jnp.int32, (rows, row.shape[1]), 0)
    row = jnp.broadcast_to(row, at.shape)
    main = row.astype(bf16).astype(f32)
    return jnp.where(at == first, main, jnp.where(at == first + 1, row - main, 0.0))


def gradients_body(pieces, place, slots, dense_ref, grad_ref, grad_t, weight_ref, *rest):
    count = len(pieces)
    tables = rest[:count]
    sums_ref, du_ref, keep_ref, send_ref = rest[count:count + 4]
    table, dense, probe, prod, mixed, vec, total, sem = rest[count + 4:]
    blocks = dense.shape[0]
    depth = table.shape[2]
    abreast = prod.shape[0]

    def dense_copy(step):
        return pltpu.make_async_copy(dense_ref.at[step], dense.at[step], sem.at[count + step])

    copies = [
        pltpu.make_async_copy(t, table.at[pl.ds(first, size)], sem.at[k])
        for k, (t, (first, size)) in enumerate(zip(tables, pieces))
    ]
    for copy in copies:
        copy.start()
    lax.fori_loop(0, blocks, lambda step, carry: (dense_copy(step).start(), carry)[1], 0)
    sums_ref[...] = jnp.zeros_like(sums_ref)
    vec[...] = jnp.zeros_like(vec)

    def project(step, carry):
        nodes = pl.ds(pl.multiple_of(step * BLK, BLK), BLK)
        probe[nodes, :] = lax.dot_general(
            grad_ref[nodes, :], weight_ref[...], (((1,), (1,)), ((), ())),
            preferred_element_type=f32,
        ).astype(bf16)
        return carry

    lax.fori_loop(0, blocks, project, 0)
    for copy in copies:
        copy.wait()

    def group(first, carry):
        steps = [first * abreast + u for u in range(abreast)]
        means = []
        for u, step in enumerate(steps):
            dense_copy(step).wait()
            row = probe[pl.ds(pl.multiple_of(step * BLK, BLK), BLK), :]
            inner = jnp.zeros((BLK, BLK), f32)
            sized = jnp.zeros((BLK, BLK), f32)
            for s in range(NBL):
                cols = slice(s * BLK, (s + 1) * BLK)
                d = lax.dot_general(
                    row, table[slots[step, s]], (((1,), (1,)), ((), ())),
                    preferred_element_type=f32,
                )
                prod[u, :, cols] = d
                a = jnp.abs(dense[step, :, cols])
                inner = inner + a * d
                sized = sized + a
            means.append(
                jnp.sum(inner, axis=1, keepdims=True) / jnp.sum(sized, axis=1, keepdims=True)
            )
        for u, step in enumerate(steps):
            du = jnp.zeros((BLK, BLK), f32)
            mix = jnp.zeros((BLK + 16, depth), f32)
            for first in range(0, NBL, JOINED):
                lhs, rhs = [], []
                for s in range(first, first + JOINED):
                    cols = slice(s * BLK, (s + 1) * BLK)
                    a = dense[step, :, cols]
                    dz = jnp.maximum(a, -0.2 * a) * (prod[u, :, cols] - means[u])
                    du = du + dz
                    slot = slots[step, s]
                    sums = jnp.sum(dz, axis=0, keepdims=True)
                    sums_ref[pl.ds(slot, 1)] += sums[None]
                    lhs.append(
                        jnp.concatenate(
                            [jnp.abs(a).astype(bf16), two_terms(sums, 0, 16).astype(bf16)], axis=0
                        )
                    )
                    rhs.append(table[slot])
                mix = mix + jnp.dot(
                    jnp.concatenate(lhs, axis=1), jnp.concatenate(rhs, axis=0),
                    preferred_element_type=f32,
                )
            row = jnp.broadcast_to(jnp.sum(du, axis=1, keepdims=True), (BLK, BLK)).T[0:1, :]
            du_ref[pl.ds(step, 1)] = row[None]
            mixed[step] = mix[:BLK].astype(bf16)
            vec[...] += mix[BLK:] + jnp.dot(
                two_terms(row, 2, 16).astype(bf16), table[step], preferred_element_type=f32
            )
        return carry

    lax.fori_loop(0, blocks // abreast, group, 0)
    lhs = jnp.concatenate([grad_t[b] for b in range(blocks)], axis=1)
    rhs = mixed[...].reshape(blocks * BLK, depth)
    total[...] = jnp.dot(lhs, rhs, preferred_element_type=f32)
    across = depth // LANES
    chunks = keep_ref.shape[0] // CHUNK
    for q in range(2 * chunks):
        r, c = q // across * CHUNK, q % across * LANES
        p = place[q]
        tile = total[r:r + CHUNK, c:c + LANES]

        @pl.when(p < chunks)
        def _():
            keep_ref[pl.ds(pl.multiple_of(p * CHUNK, CHUNK), CHUNK), :] = tile

        @pl.when(p >= chunks)
        def _():
            send_ref[pl.ds(pl.multiple_of((p - chunks) * CHUNK, CHUNK), CHUNK), :] = tile

    ends = jnp.concatenate(
        [
            (vec[r:r + 1, :] + vec[r + 1:r + 2, :])[:, c * LANES:(c + 1) * LANES]
            for r in (2, 0)
            for c in range(across)
        ],
        axis=0,
    )
    keep_ref[chunks * CHUNK:, :] = ends
    send_ref[chunks * CHUNK:, :] = ends


def gradients(place, slots, dense, grad, grad_t, weight, pieces, tables):
    blocks = dense.shape[0]
    width = grad.shape[1]
    depth = weight.shape[0]
    count = 9 * blocks
    message = (width * depth // (2 * LANES) + 8, LANES)
    return pl.pallas_call(
        functools.partial(gradients_body, pieces),
        grid_spec=pltpu.PrefetchScalarGridSpec(
            num_scalar_prefetch=2,
            grid=(1,),
            in_specs=[pl.BlockSpec(memory_space=pl.ANY)]
            + [fixed(a.shape) for a in (grad, grad_t, weight)]
            + [pl.BlockSpec(memory_space=pl.ANY)] * len(tables),
            out_specs=[
                fixed((count, 1, BLK)), fixed((blocks, 1, BLK)), fixed(message), fixed(message)
            ],
            scratch_shapes=[
                pltpu.VMEM((count, BLK, depth), bf16),
                pltpu.VMEM(dense.shape, f32),
                pltpu.VMEM(grad.shape[:1] + (depth,), bf16),
                pltpu.VMEM((2, BLK, NBL * BLK), f32),
                pltpu.VMEM((blocks, BLK, depth), bf16),
                pltpu.VMEM((16, depth), f32),
                pltpu.VMEM((width, depth), f32),
                pltpu.SemaphoreType.DMA((len(tables) + blocks,)),
            ],
        ),
        out_shape=[
            jax.ShapeDtypeStruct((count, 1, BLK), f32),
            jax.ShapeDtypeStruct((blocks, 1, BLK), f32),
            jax.ShapeDtypeStruct(message, f32),
            jax.ShapeDtypeStruct(message, f32),
        ],
        compiler_params=pltpu.CompilerParams(
            dimension_semantics=("arbitrary",), vmem_limit_bytes=60 * MIB
        ),
        cost_estimate=pl.CostEstimate(flops=0, bytes_accessed=0, transcendentals=0),
        name="gradients",
    )(place, slots, dense, grad, grad_t, weight, *tables)


def columns_of(row):
    return jnp.broadcast_to(row, (LANES, row.shape[1])).T


def finish_weight_body(scale, place, near_ref, away_ref, vec_ref, src_ref, dst_ref, weight_ref,
                       out_ref, grad_src_ref, grad_dst_ref, total):
    across = total.shape[1] // LANES
    chunks = near_ref.shape[0]
    for q in range(2 * chunks):
        r, c = q // across * CHUNK, q % across * LANES
        p = place[q]
        at = lax.rem(p, chunks)
        tile = jnp.where(p < chunks, near_ref[at].astype(f32), away_ref[at].astype(f32))
        total[r:r + CHUNK, c:c + LANES] = tile
    rows = [
        jnp.concatenate([vec_ref[v * across + c][None] for c in range(across)], axis=1)
        for v in range(2)
    ]
    full = total[...]
    for ref, row in zip((src_ref, dst_ref), rows):
        full = full + jnp.concatenate([columns_of(ref[...])] * across, axis=1) * row
    out_ref[...] = full.T * scale
    terms = [two_terms(rows[0], 0, 16), two_terms(rows[1], 2, 16)]
    for v, row in enumerate(rows):
        main = row.astype(bf16).astype(f32)
        last = row - main
        last = last - last.astype(bf16).astype(f32)
        at = lax.broadcasted_iota(jnp.int32, (16, row.shape[1]), 0)
        terms.append(jnp.where(at == 4 + v, last, 0.0))
    lhs = sum(terms[1:], terms[0]).astype(bf16)
    out = jnp.dot(lhs, weight_ref[...], preferred_element_type=f32) * scale
    grad_src_ref[...] = (out[0:1, :] + out[1:2, :] + out[4:5, :]).reshape(out.shape[1])
    grad_dst_ref[...] = (out[2:3, :] + out[3:4, :] + out[5:6, :]).reshape(out.shape[1])


def finish_weight(place, near, away, vec, src, dst, weight, scale):
    depth, width = weight.shape
    whole = lambda shape: pl.BlockSpec(shape, lambda i, p: (0,) * len(shape))
    args = (near, away, vec, src, dst, weight)
    return pl.pallas_call(
        functools.partial(finish_weight_body, scale),
        grid_spec=pltpu.PrefetchScalarGridSpec(
            num_scalar_prefetch=1,
            grid=(1,),
            in_specs=[whole(a.shape) for a in args],
            out_specs=[whole((depth, width)), whole((width,)), whole((width,))],
            scratch_shapes=[pltpu.VMEM((width, depth), f32)],
        ),
        out_shape=[
            jax.ShapeDtypeStruct((depth, width), f32),
            jax.ShapeDtypeStruct((width,), f32),
            jax.ShapeDtypeStruct((width,), f32),
        ],
        compiler_params=pltpu.CompilerParams(
            dimension_semantics=("arbitrary",), vmem_limit_bytes=60 * MIB
        ),
        name="finish_weight",
    )(place, *args)


def finish_features_body(own_ref, twin_ref, far_ref, above_ref, below_ref, du_ref, sums_ref,
                         src_ref, dst_ref, weight_ref, out_ref, src_cols, dst_cols):
    @pl.when(pl.program_id(0) == 0)
    def _():
        src_cols[...] = columns_of(src_ref[...])
        dst_cols[...] = columns_of(dst_ref[...])

    width = own_ref.shape[1]
    for k in range(du_ref.shape[0]):
        total = own_ref[k] + twin_ref[k].astype(f32) + far_ref[k].astype(f32)
        sums = sums_ref[k]
        for ref in (above_ref, below_ref):
            total = total + ref[k, :width].astype(f32)
            carried = ref[k, width:width + 16].astype(f32)
            sums = sums + carried[0:1] + carried[1:2] + carried[2:3]
        total = total + src_cols[...] * du_ref[k] + dst_cols[...] * sums
        out_ref[k * BLK:(k + 1) * BLK, :] = lax.dot_general(
            total.T.astype(bf16), weight_ref[...], (((1,), (1,)), ((), ())),
            preferred_element_type=f32,
        ).astype(bf16)


def finish_features(own, twin, far, above, below, du, sums, src, dst, weight):
    blocks = du.shape[0]
    depth, width = weight.shape
    group = blocks // 2
    tile = lambda array: pl.BlockSpec((group,) + array.shape[1:], lambda b: (b, 0, 0))
    line = pl.BlockSpec((1, width), lambda b: (0, 0))
    arrays = [own, twin, far, above, below, du, sums]
    return pl.pallas_call(
        finish_features_body,
        grid=(blocks // group,),
        in_specs=[tile(array) for array in arrays] + [line] * 2
        + [pl.BlockSpec(weight.shape, lambda b: (0, 0))],
        out_specs=pl.BlockSpec((group * BLK, depth), lambda b: (b, 0)),
        scratch_shapes=[pltpu.VMEM((width, BLK), f32)] * 2,
        out_shape=jax.ShapeDtypeStruct((blocks * BLK, depth), bf16),
        compiler_params=pltpu.CompilerParams(
            dimension_semantics=("arbitrary",), vmem_limit_bytes=60 * MIB
        ),
        cost_estimate=pl.CostEstimate(
            flops=6 * 10**9, bytes_accessed=MIB, transcendentals=0
        ),
        name="finish_features",
    )(*arrays, src, dst, weight)


def ring(axis, low, count, offset):
    size = lax.axis_size(axis)
    turned = lambda i: ((i >> low) + offset) % count - (i >> low) % count
    return [(i, i + (turned(i) << low)) for i in range(size)]


def turned(array, stage):
    axis, low, count = stage
    return [lax.ppermute(array, axis, ring(axis, low, count, k)) for k in range(1, count)]


def three_terms(array, axis):
    main = array.astype(bf16)
    rest = array - main.astype(f32)
    second = rest.astype(bf16)
    last = (rest - second.astype(f32)).astype(bf16)
    return jnp.concatenate([main, second, last], axis=axis)


def scattered(array, stage, tail, low=False):
    axis, start, count = stage
    rows = (array.shape[0] - tail) // count
    ends = array[count * rows:]
    total = [array[:rows], ends]
    for k in range(1, count):
        chunk = array[k * rows:(k + 1) * rows]
        if low:
            message = jnp.concatenate(
                [chunk.astype(bf16), three_terms(ends, 0), jnp.zeros((tail, LANES), bf16)]
            )
        else:
            message = jnp.concatenate([chunk, ends])
        came = lax.ppermute(message, axis, ring(axis, start, count, k)).astype(f32)
        total[0] = total[0] + came[:rows]
        for r in range(rows, rows + (3 if low else 1) * tail, tail):
            total[1] = total[1] + came[r:r + tail]
    return jnp.concatenate(total)


def after(array, *others):
    return lax.optimization_barrier((array, *others))[0]


def crossed(first, second, size):
    return [(a * size + c, b * size + d) for a, b in first for c, d in second]


def places(stages, sign):
    chunk = jnp.arange(math.prod(n for _, _, n in stages), dtype=jnp.int32)
    place, stride = jnp.zeros_like(chunk), 1
    for axis, low, count in stages[::-1]:
        here = (lax.axis_index(axis) >> low) % count
        place = place + (sign * (chunk // stride % count - here)) % count * stride
        stride = stride * count
    return place


def on_device(features, weight, attn_src, attn_dst, upstream, scores, neighbour_lists, edge_index):
    rows, depth = features.shape
    width = weight.shape[1]
    blocks = rows // BLK
    size_x = lax.axis_size("gx")
    size_y = lax.axis_size("gy")
    here_x = lax.axis_index("gx")
    here_y = lax.axis_index("gy")
    twin = [(i, i ^ 1) for i in range(size_x)]
    far = [(i, (((i + 1) ^ 1) - 1) % size_x) for i in range(size_x)]
    up = [(i, (i + 1) % size_y) for i in range(size_y)]
    down = [(i, (i - 1) % size_y) for i in range(size_y)]

    owner = neighbour_lists // blocks
    owner_x, owner_y = owner // size_y, owner % size_y
    part_x = jnp.where(owner_x == here_x, 0, jnp.where(owner_x // 2 == here_x // 2, 1, 2))
    part_y = jnp.where(owner_y == here_y, 0, jnp.where(owner_y == (here_y + 1) % size_y, 1, 2))
    slots = (part_x * 3 + part_y) * blocks + neighbour_lists % blocks

    own = features.reshape(blocks, BLK, depth)
    above = lax.ppermute(own, "gy", down)
    below = lax.ppermute(own, "gy", up)
    away = lax.ppermute(own, "gx", far)
    from_y = [lax.ppermute(own, ("gx", "gy"), crossed(far, way, size_y)) for way in (down, up)]
    dense, acc_own, twin_o, acc_twin, far_o, acc_far, grad_t = spread(
        slots, scores.T, edge_index.T, upstream
    )
    away, *from_y, dense, acc_own, acc_twin, acc_far, own_late = lax.optimization_barrier(
        (away, *from_y, dense, acc_own, acc_twin, acc_far, own)
    )
    across = lax.ppermute(own_late, "gx", twin)
    above, below, across = lax.optimization_barrier((above, below, across))
    sides = [across] + [lax.ppermute(t, "gx", twin) for t in (above, below)]
    from_far = lax.ppermute(acc_far, "gx", far)
    from_twin = lax.ppermute(acc_twin, "gx", twin)
    tables = [own, above, below, *sides, away, *from_y]
    pieces = tuple((k * blocks, blocks) for k in range(9))

    core, along_y, along_z = ("gx", 0, 2), ("gy", 0, 4), ("gx", 1, size_x // 2)
    stages = (core, along_y, along_z)
    sums, du, keep, send = gradients(
        places(stages, 1), slots, dense, upstream, grad_t, weight, pieces, tables
    )
    sums, du, keep, send, from_far, from_twin = lax.optimization_barrier(
        (sums, du, keep, send, from_far, from_twin)
    )
    sums = sums.reshape(3, 3, blocks, 1, BLK)
    part = keep + lax.ppermute(send, "gx", twin)

    part, sums = lax.optimization_barrier((part, sums))
    sums = sums[0] + lax.ppermute(sums[1], "gx", twin) + lax.ppermute(sums[2], "gx", far)

    def column(k):
        rows = slice((k - 1) * blocks, k * blocks)
        total = acc_own[k * blocks:(k + 1) * blocks] + from_twin[rows].astype(f32)
        total = total + from_far[rows].astype(f32)
        terms = jnp.pad(three_terms(sums[k], 1), ((0, 0), (0, 13), (0, 0)))
        return jnp.concatenate([total.astype(bf16), terms], axis=1)

    part = scattered(part, along_y, 8, low=True)
    part, to_above, to_below = lax.optimization_barrier((part, column(1), column(2)))
    from_below = lax.ppermute(to_above, "gy", up)
    from_above = lax.ppermute(to_below, "gy", down)
    part = scattered(part, along_z, 8)
    part, far_o, twin_o = lax.optimization_barrier((part, far_o, twin_o))
    from_far_o = lax.ppermute(far_o, "gx", far)
    from_twin_o = lax.ppermute(twin_o, "gx", twin)
    part, from_below, from_above, from_far_o, from_twin_o = lax.optimization_barrier(
        (part, from_below, from_above, from_far_o, from_twin_o)
    )
    part = sum(turned(part, ("gy", 2, size_y // 4)), part)
    vec = part[CHUNK:]
    part = part[:CHUNK].astype(bf16)
    part = jnp.stack([part] + turned(part, along_z))
    part, du = lax.optimization_barrier((part, du))
    part = jnp.concatenate([part] + turned(part, along_y))
    src, dst = attn_src[None], attn_dst[None]
    grad_features = finish_features(
        acc_own, from_twin_o, from_far_o, from_above, from_below, du, sums[0], src, dst, weight
    )
    part, grad_features = lax.optimization_barrier((part, grad_features))
    scale = 1.0 / math.sqrt(rows * size_x * size_y)
    grad_weight, grad_src, grad_dst = finish_weight(
        places(stages, -1), part, lax.ppermute(part, "gx", twin), vec, src, dst, weight, scale
    )
    return (grad_features, grad_weight, grad_src, grad_dst)


def solution(mesh):
    rows = P(("gx", "gy"), None)
    return jax.shard_map(
        on_device,
        mesh=mesh,
        in_specs=(rows, P(), P(), P(), rows, rows, rows, rows),
        out_specs=(rows, P(), P(), P()),
        check_vma=False,
    )
```

```python
import functools
import math

import jax
import jax.numpy as jnp
from jax import lax
from jax.experimental import pallas as pl
from jax.experimental.pallas import tpu as pltpu
from jax.sharding import PartitionSpec as P

BLK = 128
NBL = 16
WIDE = 256
HALVES = NBL * BLK // WIDE
LANES = 128
CHUNK = 256
JOINED = 4
MIB = 1 << 20

f32 = jnp.float32
bf16 = jnp.bfloat16


def spread_body(edges, slots, score_ref, index_ref, grad_ref, dense_ref, own_ref, twin_o_ref,
                twin_ref, far_o_ref, far_ref, grad_t, left_scr, right_scr, low_scr, high_scr, main_scr, rest_scr, dense,
                acc, sem):
    blocks = dense.shape[0]
    pad = ((0, LANES - edges), (0, 0))
    lanes = lax.broadcasted_iota(jnp.int32, (edges, LANES), 1).astype(f32).astype(bf16)
    halves = lax.broadcasted_iota(jnp.int32, (HALVES, LANES), 0).astype(f32)
    one = jnp.ones((edges, LANES), bf16)
    none = jnp.zeros((edges, LANES), bf16)
    tail = jnp.zeros((LANES - edges, WIDE), bf16)
    acc[...] = jnp.zeros_like(acc)
    score = score_ref[...]
    logit = jnp.where(score > 0, score, 0.2 * score)
    expo = jnp.exp(logit - jnp.max(logit, axis=0, keepdims=True))
    alpha = expo / jnp.sum(expo, axis=0, keepdims=True)
    main = alpha.astype(bf16).astype(f32)
    rest = (alpha - main).astype(bf16).astype(f32)
    index = index_ref[...]
    low_scr[...] = (index % WIDE).astype(f32)
    high = jnp.pad((index // WIDE).astype(f32), pad, constant_values=-1.0)
    main = jnp.pad(jnp.where(score > 0, main, -main), pad)
    rest = jnp.pad(jnp.where(score > 0, rest, -rest), pad)
    for b in range(blocks):
        nodes = slice(b * BLK, (b + 1) * BLK)
        high_scr[nodes, :] = high[:, nodes].T
        main_scr[nodes, :] = main[:, nodes].T
        rest_scr[nodes, :] = rest[:, nodes].T
        grad_t[b] = grad_ref[nodes, :].T

    def out_copy(step):
        return pltpu.make_async_copy(dense.at[step], dense_ref.at[step], sem.at[step])

    def block(step, carry):
        nodes = pl.ds(pl.multiple_of(step * BLK, BLK), BLK)
        low = low_scr[:, nodes]
        high, main, rest = high_scr[nodes, :], main_scr[nodes, :], rest_scr[nodes, :]
        for i in range(BLK):
            here = jnp.broadcast_to(high[i:i + 1, :], (HALVES, LANES)) == halves
            lhs = jnp.concatenate(
                [
                    jnp.where(here, jnp.broadcast_to(term[i:i + 1, :], (HALVES, LANES)), 0.0)
                    for term in (main, rest)
                ],
                axis=0,
            ).astype(bf16)
            column = jnp.broadcast_to(low[:, i:i + 1], (edges, LANES)).astype(bf16)
            rhs = jnp.concatenate(
                [jnp.where(column == lanes + LANES * c, one, none) for c in range(WIDE // LANES)],
                axis=1,
            )
            rhs = jnp.concatenate([rhs, tail], axis=0)
            out = jnp.dot(lhs, rhs, preferred_element_type=f32)
            left_scr[2 * HALVES * i:2 * HALVES * (i + 1), :] = out[:, :LANES]
            right_scr[2 * HALVES * i:2 * HALVES * (i + 1), :] = out[:, LANES:]
        for s in range(NBL):
            scr = (left_scr, right_scr)[s % 2]
            main = scr[pl.ds(s // 2, BLK, stride=2 * HALVES), :]
            rest = scr[pl.ds(HALVES + s // 2, BLK, stride=2 * HALVES), :]
            dense[step, :, s * BLK:(s + 1) * BLK] = main + rest
            low = jnp.abs(main).astype(bf16)
            term = jnp.dot(grad_t[step], low, preferred_element_type=f32)[None]
            acc[pl.ds(slots[step, s], 1)] += term
        out_copy(step).start()
        return carry

    lax.fori_loop(0, blocks, block, 0)
    per = own_ref.shape[0]

    def cast(k, carry):
        own_ref[pl.ds(k, 1)] = acc[pl.ds(2 * per + k, 1)]
        return carry

    def cast_own(k, carry):
        twin_o_ref[pl.ds(k, 1)] = acc[pl.ds(k, 1)].astype(bf16)
        far_o_ref[pl.ds(k, 1)] = acc[pl.ds(per + k, 1)].astype(bf16)
        return carry

    def cast_sides(k, carry):
        twin_ref[pl.ds(k, 1)] = acc[pl.ds(blocks + k, 1)].astype(bf16)
        far_ref[pl.ds(k, 1)] = acc[pl.ds(per + blocks + k, 1)].astype(bf16)
        return carry

    lax.fori_loop(0, per, cast, 0)
    lax.fori_loop(0, blocks, cast_own, 0)
    lax.fori_loop(0, per - blocks, cast_sides, 0)
    lax.fori_loop(0, blocks, lambda step, carry: (out_copy(step).wait(), carry)[1], 0)


def fixed(shape):
    return pl.BlockSpec(shape, lambda *_: (0,) * len(shape), pipeline_mode=pl.Buffered(1))


def spread(slots, scores, index, grad):
    edges, rows = scores.shape
    blocks = rows // BLK
    width = grad.shape[1]
    per = 3 * blocks
    away = [(blocks, width, BLK), (2 * blocks, width, BLK)]
    sums = [(per, width, BLK)] + away + away + [(blocks, width, BLK)]
    types = [f32] + [bf16] * 5
    dense = (blocks, BLK, NBL * BLK)
    return pl.pallas_call(
        functools.partial(spread_body, edges),
        grid_spec=pltpu.PrefetchScalarGridSpec(
            num_scalar_prefetch=1,
            grid=(1,),
            in_specs=[fixed(scores.shape), fixed(index.shape), fixed(grad.shape)],
            out_specs=[pl.BlockSpec(memory_space=pl.ANY)] + [fixed(shape) for shape in sums],
            scratch_shapes=[
                pltpu.VMEM((2 * HALVES * BLK, LANES), f32),
                pltpu.VMEM((2 * HALVES * BLK, LANES), f32),
                pltpu.VMEM((edges, rows), f32),
                pltpu.VMEM((rows, LANES), f32),
                pltpu.VMEM((rows, LANES), f32),
                pltpu.VMEM((rows, LANES), f32),
                pltpu.VMEM(dense, f32),
                pltpu.VMEM((3 * per, width, BLK), f32),
                pltpu.SemaphoreType.DMA((blocks,)),
            ],
        ),
        out_shape=[jax.ShapeDtypeStruct(dense, f32)]
        + [jax.ShapeDtypeStruct(*pair) for pair in zip(sums, types)],
        compiler_params=pltpu.CompilerParams(
            dimension_semantics=("arbitrary",), vmem_limit_bytes=60 * MIB
        ),
        cost_estimate=pl.CostEstimate(flops=0, bytes_accessed=0, transcendentals=0),
        name="spread",
    )((slots + 2 * per) % (3 * per), scores, index, grad)


def two_terms(row, first, rows):
    at = lax.broadcasted_iota(jnp.int32, (rows, row.shape[1]), 0)
    row = jnp.broadcast_to(row, at.shape)
    main = row.astype(bf16).astype(f32)
    return jnp.where(at == first, main, jnp.where(at == first + 1, row - main, 0.0))


def gradients_body(pieces, place, slots, dense_ref, grad_ref, grad_t, weight_ref, *rest):
    count = len(pieces)
    tables = rest[:count]
    sums_ref, du_ref, keep_ref, send_ref = rest[count:count + 4]
    table, dense, probe, prod, mixed, vec, total, sem = rest[count + 4:]
    blocks = dense.shape[0]
    depth = table.shape[2]
    abreast = prod.shape[0]

    def dense_copy(step):
        return pltpu.make_async_copy(dense_ref.at[step], dense.at[step], sem.at[count + step])

    copies = [
        pltpu.make_async_copy(t, table.at[pl.ds(first, size)], sem.at[k])
        for k, (t, (first, size)) in enumerate(zip(tables, pieces))
    ]
    for copy in copies:
        copy.start()
    lax.fori_loop(0, blocks, lambda step, carry: (dense_copy(step).start(), carry)[1], 0)
    sums_ref[...] = jnp.zeros_like(sums_ref)
    vec[...] = jnp.zeros_like(vec)

    def project(step, carry):
        nodes = pl.ds(pl.multiple_of(step * BLK, BLK), BLK)
        probe[nodes, :] = lax.dot_general(
            grad_ref[nodes, :], weight_ref[...], (((1,), (1,)), ((), ())),
            preferred_element_type=f32,
        ).astype(bf16)
        return carry

    lax.fori_loop(0, blocks, project, 0)
    for copy in copies:
        copy.wait()

    def group(first, carry):
        steps = [first * abreast + u for u in range(abreast)]
        means = []
        for u, step in enumerate(steps):
            dense_copy(step).wait()
            row = probe[pl.ds(pl.multiple_of(step * BLK, BLK), BLK), :]
            inner = jnp.zeros((BLK, BLK), f32)
            sized = jnp.zeros((BLK, BLK), f32)
            for s in range(NBL):
                cols = slice(s * BLK, (s + 1) * BLK)
                d = lax.dot_general(
                    row, table[slots[step, s]], (((1,), (1,)), ((), ())),
                    preferred_element_type=f32,
                )
                prod[u, :, cols] = d
                a = jnp.abs(dense[step, :, cols])
                inner = inner + a * d
                sized = sized + a
            means.append(
                jnp.sum(inner, axis=1, keepdims=True) / jnp.sum(sized, axis=1, keepdims=True)
            )
        for u, step in enumerate(steps):
            du = jnp.zeros((BLK, BLK), f32)
            mix = jnp.zeros((BLK + 16, depth), f32)
            for first in range(0, NBL, JOINED):
                lhs, rhs = [], []
                for s in range(first, first + JOINED):
                    cols = slice(s * BLK, (s + 1) * BLK)
                    a = dense[step, :, cols]
                    dz = jnp.maximum(a, -0.2 * a) * (prod[u, :, cols] - means[u])
                    du = du + dz
                    slot = slots[step, s]
                    sums = jnp.sum(dz, axis=0, keepdims=True)
                    sums_ref[pl.ds(slot, 1)] += sums[None]
                    lhs.append(
                        jnp.concatenate(
                            [jnp.abs(a).astype(bf16), two_terms(sums, 0, 16).astype(bf16)], axis=0
                        )
                    )
                    rhs.append(table[slot])
                mix = mix + jnp.dot(
                    jnp.concatenate(lhs, axis=1), jnp.concatenate(rhs, axis=0),
                    preferred_element_type=f32,
                )
            row = jnp.broadcast_to(jnp.sum(du, axis=1, keepdims=True), (BLK, BLK)).T[0:1, :]
            du_ref[pl.ds(step, 1)] = row[None]
            mixed[step] = mix[:BLK].astype(bf16)
            vec[...] += mix[BLK:] + jnp.dot(
                two_terms(row, 2, 16).astype(bf16), table[step], preferred_element_type=f32
            )
        return carry

    lax.fori_loop(0, blocks // abreast, group, 0)
    lhs = jnp.concatenate([grad_t[b] for b in range(blocks)], axis=1)
    rhs = mixed[...].reshape(blocks * BLK, depth)
    total[...] = jnp.dot(lhs, rhs, preferred_element_type=f32)
    across = depth // LANES
    chunks = keep_ref.shape[0] // CHUNK
    for q in range(2 * chunks):
        r, c = q // across * CHUNK, q % across * LANES
        p = place[q]
        tile = total[r:r + CHUNK, c:c + LANES]

        @pl.when(p < chunks)
        def _():
            keep_ref[pl.ds(pl.multiple_of(p * CHUNK, CHUNK), CHUNK), :] = tile

        @pl.when(p >= chunks)
        def _():
            send_ref[pl.ds(pl.multiple_of((p - chunks) * CHUNK, CHUNK), CHUNK), :] = tile

    ends = jnp.concatenate(
        [
            (vec[r:r + 1, :] + vec[r + 1:r + 2, :])[:, c * LANES:(c + 1) * LANES]
            for r in (2, 0)
            for c in range(across)
        ],
        axis=0,
    )
    keep_ref[chunks * CHUNK:, :] = ends
    send_ref[chunks * CHUNK:, :] = ends


def gradients(place, slots, dense, grad, grad_t, weight, pieces, tables):
    blocks = dense.shape[0]
    width = grad.shape[1]
    depth = weight.shape[0]
    count = 9 * blocks
    message = (width * depth // (2 * LANES) + 8, LANES)
    return pl.pallas_call(
        functools.partial(gradients_body, pieces),
        grid_spec=pltpu.PrefetchScalarGridSpec(
            num_scalar_prefetch=2,
            grid=(1,),
            in_specs=[pl.BlockSpec(memory_space=pl.ANY)]
            + [fixed(a.shape) for a in (grad, grad_t, weight)]
            + [pl.BlockSpec(memory_space=pl.ANY)] * len(tables),
            out_specs=[
                fixed((count, 1, BLK)), fixed((blocks, 1, BLK)), fixed(message), fixed(message)
            ],
            scratch_shapes=[
                pltpu.VMEM((count, BLK, depth), bf16),
                pltpu.VMEM(dense.shape, f32),
                pltpu.VMEM(grad.shape[:1] + (depth,), bf16),
                pltpu.VMEM((2, BLK, NBL * BLK), f32),
                pltpu.VMEM((blocks, BLK, depth), bf16),
                pltpu.VMEM((16, depth), f32),
                pltpu.VMEM((width, depth), f32),
                pltpu.SemaphoreType.DMA((len(tables) + blocks,)),
            ],
        ),
        out_shape=[
            jax.ShapeDtypeStruct((count, 1, BLK), f32),
            jax.ShapeDtypeStruct((blocks, 1, BLK), f32),
            jax.ShapeDtypeStruct(message, f32),
            jax.ShapeDtypeStruct(message, f32),
        ],
        compiler_params=pltpu.CompilerParams(
            dimension_semantics=("arbitrary",), vmem_limit_bytes=60 * MIB
        ),
        cost_estimate=pl.CostEstimate(flops=0, bytes_accessed=0, transcendentals=0),
        name="gradients",
    )(place, slots, dense, grad, grad_t, weight, *tables)


def columns_of(row):
    return jnp.broadcast_to(row, (LANES, row.shape[1])).T


def finish_weight_body(scale, place, near_ref, away_ref, vec_ref, src_ref, dst_ref, weight_ref,
                       out_ref, grad_src_ref, grad_dst_ref, total):
    across = total.shape[1] // LANES
    chunks = near_ref.shape[0]
    for q in range(2 * chunks):
        r, c = q // across * CHUNK, q % across * LANES
        p = place[q]
        at = lax.rem(p, chunks)
        tile = jnp.where(p < chunks, near_ref[at].astype(f32), away_ref[at].astype(f32))
        total[r:r + CHUNK, c:c + LANES] = tile
    rows = [
        jnp.concatenate([vec_ref[v * across + c][None] for c in range(across)], axis=1)
        for v in range(2)
    ]
    full = total[...]
    for ref, row in zip((src_ref, dst_ref), rows):
        full = full + jnp.concatenate([columns_of(ref[...])] * across, axis=1) * row
    out_ref[...] = full.T * scale
    terms = [two_terms(rows[0], 0, 16), two_terms(rows[1], 2, 16)]
    for v, row in enumerate(rows):
        main = row.astype(bf16).astype(f32)
        last = row - main
        last = last - last.astype(bf16).astype(f32)
        at = lax.broadcasted_iota(jnp.int32, (16, row.shape[1]), 0)
        terms.append(jnp.where(at == 4 + v, last, 0.0))
    lhs = sum(terms[1:], terms[0]).astype(bf16)
    out = jnp.dot(lhs, weight_ref[...], preferred_element_type=f32) * scale
    grad_src_ref[...] = (out[0:1, :] + out[1:2, :] + out[4:5, :]).reshape(out.shape[1])
    grad_dst_ref[...] = (out[2:3, :] + out[3:4, :] + out[5:6, :]).reshape(out.shape[1])


def finish_weight(place, near, away, vec, src, dst, weight, scale):
    depth, width = weight.shape
    whole = lambda shape: pl.BlockSpec(shape, lambda i, p: (0,) * len(shape))
    args = (near, away, vec, src, dst, weight)
    return pl.pallas_call(
        functools.partial(finish_weight_body, scale),
        grid_spec=pltpu.PrefetchScalarGridSpec(
            num_scalar_prefetch=1,
            grid=(1,),
            in_specs=[whole(a.shape) for a in args],
            out_specs=[whole((depth, width)), whole((width,)), whole((width,))],
            scratch_shapes=[pltpu.VMEM((width, depth), f32)],
        ),
        out_shape=[
            jax.ShapeDtypeStruct((depth, width), f32),
            jax.ShapeDtypeStruct((width,), f32),
            jax.ShapeDtypeStruct((width,), f32),
        ],
        compiler_params=pltpu.CompilerParams(
            dimension_semantics=("arbitrary",), vmem_limit_bytes=60 * MIB
        ),
        name="finish_weight",
    )(place, *args)


def finish_features_body(own_ref, twin_ref, far_ref, above_ref, below_ref, du_ref, sums_ref,
                         src_ref, dst_ref, weight_ref, out_ref, src_cols, dst_cols):
    @pl.when(pl.program_id(0) == 0)
    def _():
        src_cols[...] = columns_of(src_ref[...])
        dst_cols[...] = columns_of(dst_ref[...])

    width = own_ref.shape[1]
    for k in range(du_ref.shape[0]):
        total = own_ref[k] + twin_ref[k].astype(f32) + far_ref[k].astype(f32)
        sums = sums_ref[k]
        for ref in (above_ref, below_ref):
            total = total + ref[k, :width].astype(f32)
            carried = ref[k, width:width + 16].astype(f32)
            sums = sums + carried[0:1] + carried[1:2] + carried[2:3]
        total = total + src_cols[...] * du_ref[k] + dst_cols[...] * sums
        out_ref[k * BLK:(k + 1) * BLK, :] = lax.dot_general(
            total.T.astype(bf16), weight_ref[...], (((1,), (1,)), ((), ())),
            preferred_element_type=f32,
        ).astype(bf16)


def finish_features(own, twin, far, above, below, du, sums, src, dst, weight):
    blocks = du.shape[0]
    depth, width = weight.shape
    group = blocks // 2
    tile = lambda array: pl.BlockSpec((group,) + array.shape[1:], lambda b: (b, 0, 0))
    line = pl.BlockSpec((1, width), lambda b: (0, 0))
    arrays = [own, twin, far, above, below, du, sums]
    return pl.pallas_call(
        finish_features_body,
        grid=(blocks // group,),
        in_specs=[tile(array) for array in arrays] + [line] * 2
        + [pl.BlockSpec(weight.shape, lambda b: (0, 0))],
        out_specs=pl.BlockSpec((group * BLK, depth), lambda b: (b, 0)),
        scratch_shapes=[pltpu.VMEM((width, BLK), f32)] * 2,
        out_shape=jax.ShapeDtypeStruct((blocks * BLK, depth), bf16),
        compiler_params=pltpu.CompilerParams(
            dimension_semantics=("arbitrary",), vmem_limit_bytes=60 * MIB
        ),
        cost_estimate=pl.CostEstimate(
            flops=6 * 10**9, bytes_accessed=MIB, transcendentals=0
        ),
        name="finish_features",
    )(*arrays, src, dst, weight)


def ring(axis, low, count, offset):
    size = lax.axis_size(axis)
    turned = lambda i: ((i >> low) + offset) % count - (i >> low) % count
    return [(i, i + (turned(i) << low)) for i in range(size)]


def turned(array, stage):
    axis, low, count = stage
    return [lax.ppermute(array, axis, ring(axis, low, count, k)) for k in range(1, count)]


def three_terms(array, axis):
    main = array.astype(bf16)
    rest = array - main.astype(f32)
    second = rest.astype(bf16)
    last = (rest - second.astype(f32)).astype(bf16)
    return jnp.concatenate([main, second, last], axis=axis)


def lowered(array, ends):
    return jnp.concatenate(
        [array.astype(bf16), three_terms(ends, 0), jnp.zeros(ends.shape, bf16)]
    )


def raised(terms):
    tail = terms.shape[0] // 4
    return terms[:tail] + terms[tail:2 * tail] + terms[2 * tail:3 * tail]


def summed(array, stage):
    first, across, last = (t.astype(f32) for t in turned(array, stage))
    return (array.astype(f32) + across) + (first + last)


def scattered(array, stage, tail):
    axis, start, count = stage
    rows = (array.shape[0] - tail) // count
    ends = array[count * rows:]
    own = array[:rows]
    came = []
    for k in range(1, count):
        message = lowered(array[k * rows:(k + 1) * rows], ends)
        came.append(lax.ppermute(message, axis, ring(axis, start, count, k)).astype(f32))
    first, across, last = came
    matrix = (own + across[:rows]) + (first[:rows] + last[:rows])
    vector = (ends + raised(across[rows:])) + (raised(first[rows:]) + raised(last[rows:]))
    return jnp.concatenate([matrix, vector])


def after(array, *others):
    return lax.optimization_barrier((array, *others))[0]


def crossed(first, second, size):
    return [(a * size + c, b * size + d) for a, b in first for c, d in second]


def places(stages, sign):
    chunk = jnp.arange(math.prod(n for _, _, n in stages), dtype=jnp.int32)
    place, stride = jnp.zeros_like(chunk), 1
    for axis, low, count in stages[::-1]:
        here = (lax.axis_index(axis) >> low) % count
        place = place + (sign * (chunk // stride % count - here)) % count * stride
        stride = stride * count
    return place


def on_device(features, weight, attn_src, attn_dst, upstream, scores, neighbour_lists, edge_index):
    rows, depth = features.shape
    width = weight.shape[1]
    blocks = rows // BLK
    size_x = lax.axis_size("gx")
    size_y = lax.axis_size("gy")
    here_x = lax.axis_index("gx")
    here_y = lax.axis_index("gy")
    twin = [(i, i ^ 1) for i in range(size_x)]
    far = [(i, (((i + 1) ^ 1) - 1) % size_x) for i in range(size_x)]
    up = [(i, (i + 1) % size_y) for i in range(size_y)]
    down = [(i, (i - 1) % size_y) for i in range(size_y)]

    owner = neighbour_lists // blocks
    owner_x, owner_y = owner // size_y, owner % size_y
    part_x = jnp.where(owner_x == here_x, 0, jnp.where(owner_x // 2 == here_x // 2, 1, 2))
    part_y = jnp.where(owner_y == here_y, 0, jnp.where(owner_y == (here_y + 1) % size_y, 1, 2))
    slots = (part_x * 3 + part_y) * blocks + neighbour_lists % blocks

    own = features.reshape(blocks, BLK, depth)
    above = lax.ppermute(own, "gy", down)
    below = lax.ppermute(own, "gy", up)
    away = lax.ppermute(own, "gx", far)
    from_y = [lax.ppermute(own, ("gx", "gy"), crossed(far, way, size_y)) for way in (down, up)]
    dense, acc_own, twin_o, acc_twin, far_o, acc_far, grad_t = spread(
        slots, scores.T, edge_index.T, upstream
    )
    away, *from_y, dense, acc_own, acc_twin, acc_far, own_late = lax.optimization_barrier(
        (away, *from_y, dense, acc_own, acc_twin, acc_far, own)
    )
    across = lax.ppermute(own_late, "gx", twin)
    above, below, across = lax.optimization_barrier((above, below, across))
    sides = [across] + [lax.ppermute(t, "gx", twin) for t in (above, below)]
    from_far = lax.ppermute(acc_far, "gx", far)
    from_twin = lax.ppermute(acc_twin, "gx", twin)
    tables = [own, above, below, *sides, away, *from_y]
    pieces = tuple((k * blocks, blocks) for k in range(9))

    core, along_y, along_z = ("gx", 0, 2), ("gy", 0, 4), ("gx", 1, size_x // 2)
    stages = (core, along_y)
    sums, du, keep, send = gradients(
        places(stages, 1), slots, dense, upstream, grad_t, weight, pieces, tables
    )
    sums, du, keep, send, from_far, from_twin = lax.optimization_barrier(
        (sums, du, keep, send, from_far, from_twin)
    )
    sums = sums.reshape(3, 3, blocks, 1, BLK)
    part = keep + lax.ppermute(send, "gx", twin)

    part, sums = lax.optimization_barrier((part, sums))
    sums = sums[0] + lax.ppermute(sums[1], "gx", twin) + lax.ppermute(sums[2], "gx", far)

    def column(k):
        rows = slice((k - 1) * blocks, k * blocks)
        total = acc_own[k * blocks:(k + 1) * blocks] + from_twin[rows].astype(f32)
        total = total + from_far[rows].astype(f32)
        terms = jnp.pad(three_terms(sums[k], 1), ((0, 0), (0, 13), (0, 0)))
        return jnp.concatenate([total.astype(bf16), terms], axis=1)

    part = scattered(part, along_y, 8)
    part, sums = lax.optimization_barrier((part, sums))
    to_above, to_below = column(1), column(2)
    from_below = lax.ppermute(to_above, "gy", up)
    from_above = lax.ppermute(to_below, "gy", down)
    part = summed(part, along_z)
    part, far_o, twin_o = lax.optimization_barrier((part, far_o, twin_o))
    from_far_o = lax.ppermute(far_o, "gx", far)
    from_twin_o = lax.ppermute(twin_o, "gx", twin)
    part, from_below, from_above, from_far_o, from_twin_o = lax.optimization_barrier(
        (part, from_below, from_above, from_far_o, from_twin_o)
    )
    part = summed(lowered(part[:CHUNK], part[CHUNK:]), ("gy", 2, size_y // 4))
    vec = raised(part[CHUNK:])
    part = part[:CHUNK].astype(bf16)
    part, du = lax.optimization_barrier((part, du))
    part = part[None]
    part = jnp.concatenate([part] + turned(part, along_y))
    src, dst = attn_src[None], attn_dst[None]
    grad_features = finish_features(
        acc_own, from_twin_o, from_far_o, from_above, from_below, du, sums[0], src, dst, weight
    )
    part, grad_features = lax.optimization_barrier((part, grad_features))
    scale = 1.0 / math.sqrt(rows * size_x * size_y)
    grad_weight, grad_src, grad_dst = finish_weight(
        places(stages, -1), part, lax.ppermute(part, "gx", twin), vec, src, dst, weight, scale
    )
    return (grad_features, grad_weight, grad_src, grad_dst)


def solution(mesh):
    rows = P(("gx", "gy"), None)
    return jax.shard_map(
        on_device,
        mesh=mesh,
        in_specs=(rows, P(), P(), P(), rows, rows, rows, rows),
        out_specs=(rows, P(), P(), P()),
        check_vma=False,
    )
```

```python
import functools
import math

import jax
import jax.numpy as jnp
from jax import lax
from jax.experimental import pallas as pl
from jax.experimental.pallas import tpu as pltpu
from jax.sharding import PartitionSpec as P

BLK = 128
NBL = 16
WIDE = 256
HALVES = NBL * BLK // WIDE
LANES = 128
CHUNK = 256
JOINED = 4
MIB = 1 << 20

f32 = jnp.float32
bf16 = jnp.bfloat16


def spread_body(edges, slots, score_ref, index_ref, grad_ref, dense_ref, own_ref, twin_o_ref,
                twin_ref, far_o_ref, far_ref, grad_t, left_scr, right_scr, low_scr, high_scr, main_scr, rest_scr, dense,
                acc, sem):
    blocks = dense.shape[0]
    pad = ((0, LANES - edges), (0, 0))
    lanes = lax.broadcasted_iota(jnp.int32, (edges, LANES), 1).astype(f32).astype(bf16)
    halves = lax.broadcasted_iota(jnp.int32, (HALVES, LANES), 0).astype(f32)
    one = jnp.ones((edges, LANES), bf16)
    none = jnp.zeros((edges, LANES), bf16)
    tail = jnp.zeros((LANES - edges, WIDE), bf16)
    acc[...] = jnp.zeros_like(acc)
    score = score_ref[...]
    logit = jnp.where(score > 0, score, 0.2 * score)
    expo = jnp.exp(logit - jnp.max(logit, axis=0, keepdims=True))
    alpha = expo / jnp.sum(expo, axis=0, keepdims=True)
    main = alpha.astype(bf16).astype(f32)
    rest = (alpha - main).astype(bf16).astype(f32)
    index = index_ref[...]
    low_scr[...] = (index % WIDE).astype(f32)
    high = jnp.pad((index // WIDE).astype(f32), pad, constant_values=-1.0)
    main = jnp.pad(jnp.where(score > 0, main, -main), pad)
    rest = jnp.pad(jnp.where(score > 0, rest, -rest), pad)
    for b in range(blocks):
        nodes = slice(b * BLK, (b + 1) * BLK)
        high_scr[nodes, :] = high[:, nodes].T
        main_scr[nodes, :] = main[:, nodes].T
        rest_scr[nodes, :] = rest[:, nodes].T
        grad_t[b] = grad_ref[nodes, :].T

    def out_copy(step):
        return pltpu.make_async_copy(dense.at[step], dense_ref.at[step], sem.at[step])

    def block(step, carry):
        nodes = pl.ds(pl.multiple_of(step * BLK, BLK), BLK)
        low = low_scr[:, nodes]
        high, main, rest = high_scr[nodes, :], main_scr[nodes, :], rest_scr[nodes, :]
        for i in range(BLK):
            here = jnp.broadcast_to(high[i:i + 1, :], (HALVES, LANES)) == halves
            lhs = jnp.concatenate(
                [
                    jnp.where(here, jnp.broadcast_to(term[i:i + 1, :], (HALVES, LANES)), 0.0)
                    for term in (main, rest)
                ],
                axis=0,
            ).astype(bf16)
            column = jnp.broadcast_to(low[:, i:i + 1], (edges, LANES)).astype(bf16)
            rhs = jnp.concatenate(
                [jnp.where(column == lanes + LANES * c, one, none) for c in range(WIDE // LANES)],
                axis=1,
            )
            rhs = jnp.concatenate([rhs, tail], axis=0)
            out = jnp.dot(lhs, rhs, preferred_element_type=f32)
            left_scr[2 * HALVES * i:2 * HALVES * (i + 1), :] = out[:, :LANES]
            right_scr[2 * HALVES * i:2 * HALVES * (i + 1), :] = out[:, LANES:]
        for s in range(NBL):
            scr = (left_scr, right_scr)[s % 2]
            main = scr[pl.ds(s // 2, BLK, stride=2 * HALVES), :]
            rest = scr[pl.ds(HALVES + s // 2, BLK, stride=2 * HALVES), :]
            dense[step, :, s * BLK:(s + 1) * BLK] = main + rest
            low = jnp.abs(main).astype(bf16)
            term = jnp.dot(grad_t[step], low, preferred_element_type=f32)[None]
            acc[pl.ds(slots[step, s], 1)] += term
        out_copy(step).start()
        return carry

    lax.fori_loop(0, blocks, block, 0)
    per = own_ref.shape[0]

    def cast(k, carry):
        own_ref[pl.ds(k, 1)] = acc[pl.ds(2 * per + k, 1)]
        return carry

    def cast_own(k, carry):
        twin_o_ref[pl.ds(k, 1)] = acc[pl.ds(k, 1)].astype(bf16)
        far_o_ref[pl.ds(k, 1)] = acc[pl.ds(per + k, 1)].astype(bf16)
        return carry

    def cast_sides(k, carry):
        twin_ref[pl.ds(k, 1)] = acc[pl.ds(blocks + k, 1)].astype(bf16)
        far_ref[pl.ds(k, 1)] = acc[pl.ds(per + blocks + k, 1)].astype(bf16)
        return carry

    lax.fori_loop(0, per, cast, 0)
    lax.fori_loop(0, blocks, cast_own, 0)
    lax.fori_loop(0, per - blocks, cast_sides, 0)
    lax.fori_loop(0, blocks, lambda step, carry: (out_copy(step).wait(), carry)[1], 0)


def fixed(shape):
    return pl.BlockSpec(shape, lambda *_: (0,) * len(shape), pipeline_mode=pl.Buffered(1))


def spread(slots, scores, index, grad):
    edges, rows = scores.shape
    blocks = rows // BLK
    width = grad.shape[1]
    per = 3 * blocks
    away = [(blocks, width, BLK), (2 * blocks, width, BLK)]
    sums = [(per, width, BLK)] + away + away + [(blocks, width, BLK)]
    types = [f32] + [bf16] * 5
    dense = (blocks, BLK, NBL * BLK)
    return pl.pallas_call(
        functools.partial(spread_body, edges),
        grid_spec=pltpu.PrefetchScalarGridSpec(
            num_scalar_prefetch=1,
            grid=(1,),
            in_specs=[fixed(scores.shape), fixed(index.shape), fixed(grad.shape)],
            out_specs=[pl.BlockSpec(memory_space=pl.ANY)] + [fixed(shape) for shape in sums],
            scratch_shapes=[
                pltpu.VMEM((2 * HALVES * (BLK + 1), LANES), f32),
                pltpu.VMEM((2 * HALVES * (BLK + 1), LANES), f32),
                pltpu.VMEM((edges, rows), f32),
                pltpu.VMEM((rows, LANES), f32),
                pltpu.VMEM((rows, LANES), f32),
                pltpu.VMEM((rows, LANES), f32),
                pltpu.VMEM(dense, f32),
                pltpu.VMEM((3 * per, width, BLK), f32),
                pltpu.SemaphoreType.DMA((blocks,)),
            ],
        ),
        out_shape=[jax.ShapeDtypeStruct(dense, f32)]
        + [jax.ShapeDtypeStruct(*pair) for pair in zip(sums, types)],
        compiler_params=pltpu.CompilerParams(
            dimension_semantics=("arbitrary",), vmem_limit_bytes=60 * MIB
        ),
        cost_estimate=pl.CostEstimate(flops=0, bytes_accessed=0, transcendentals=0),
        name="spread",
    )((slots + 2 * per) % (3 * per), scores, index, grad)


def two_terms(row, first, rows):
    at = lax.broadcasted_iota(jnp.int32, (rows, row.shape[1]), 0)
    row = jnp.broadcast_to(row, at.shape)
    main = row.astype(bf16).astype(f32)
    return jnp.where(at == first, main, jnp.where(at == first + 1, row - main, 0.0))


def gradients_body(pieces, place, slots, dense_ref, grad_ref, grad_t, weight_ref, *rest):
    count = len(pieces)
    tables = rest[:count]
    sums_ref, du_ref, keep_ref, send_ref = rest[count:count + 4]
    table, dense, probe, prod, mixed, vec, total, sem = rest[count + 4:]
    blocks = dense.shape[0]
    depth = table.shape[2]
    abreast = prod.shape[0]

    def dense_copy(step):
        return pltpu.make_async_copy(dense_ref.at[step], dense.at[step], sem.at[count + step])

    copies = [
        pltpu.make_async_copy(t, table.at[pl.ds(first, size)], sem.at[k])
        for k, (t, (first, size)) in enumerate(zip(tables, pieces))
    ]
    for copy in copies:
        copy.start()
    lax.fori_loop(0, blocks, lambda step, carry: (dense_copy(step).start(), carry)[1], 0)
    sums_ref[...] = jnp.zeros_like(sums_ref)
    vec[...] = jnp.zeros_like(vec)

    def project(step, carry):
        nodes = pl.ds(pl.multiple_of(step * BLK, BLK), BLK)
        probe[nodes, :] = lax.dot_general(
            grad_ref[nodes, :], weight_ref[...], (((1,), (1,)), ((), ())),
            preferred_element_type=f32,
        ).astype(bf16)
        return carry

    lax.fori_loop(0, blocks, project, 0)
    for copy in copies:
        copy.wait()

    def group(first, carry):
        steps = [first * abreast + u for u in range(abreast)]
        means = []
        for u, step in enumerate(steps):
            dense_copy(step).wait()
            row = probe[pl.ds(pl.multiple_of(step * BLK, BLK), BLK), :]
            inner = jnp.zeros((BLK, BLK), f32)
            sized = jnp.zeros((BLK, BLK), f32)
            for s in range(NBL):
                cols = slice(s * BLK, (s + 1) * BLK)
                d = lax.dot_general(
                    row, table[slots[step, s]], (((1,), (1,)), ((), ())),
                    preferred_element_type=f32,
                )
                prod[u, :, cols] = d
                a = jnp.abs(dense[step, :, cols])
                inner = inner + a * d
                sized = sized + a
            means.append(
                jnp.sum(inner, axis=1, keepdims=True) / jnp.sum(sized, axis=1, keepdims=True)
            )
        for u, step in enumerate(steps):
            du = jnp.zeros((BLK, BLK), f32)
            mix = jnp.zeros((BLK + 16, depth), f32)
            for first in range(0, NBL, JOINED):
                lhs, rhs = [], []
                for s in range(first, first + JOINED):
                    cols = slice(s * BLK, (s + 1) * BLK)
                    a = dense[step, :, cols]
                    dz = jnp.maximum(a, -0.2 * a) * (prod[u, :, cols] - means[u])
                    du = du + dz
                    slot = slots[step, s]
                    sums = jnp.sum(dz, axis=0, keepdims=True)
                    sums_ref[pl.ds(slot, 1)] += sums[None]
                    lhs.append(
                        jnp.concatenate(
                            [jnp.abs(a).astype(bf16), two_terms(sums, 0, 16).astype(bf16)], axis=0
                        )
                    )
                    rhs.append(table[slot])
                mix = mix + jnp.dot(
                    jnp.concatenate(lhs, axis=1), jnp.concatenate(rhs, axis=0),
                    preferred_element_type=f32,
                )
            row = jnp.broadcast_to(jnp.sum(du, axis=1, keepdims=True), (BLK, BLK)).T[0:1, :]
            du_ref[pl.ds(step, 1)] = row[None]
            mixed[step] = mix[:BLK].astype(bf16)
            vec[...] += mix[BLK:] + jnp.dot(
                two_terms(row, 2, 16).astype(bf16), table[step], preferred_element_type=f32
            )
        return carry

    lax.fori_loop(0, blocks // abreast, group, 0)
    lhs = jnp.concatenate([grad_t[b] for b in range(blocks)], axis=1)
    rhs = mixed[...].reshape(blocks * BLK, depth)
    total[...] = jnp.dot(lhs, rhs, preferred_element_type=f32)
    across = depth // LANES
    chunks = keep_ref.shape[0] // CHUNK
    for q in range(2 * chunks):
        r, c = q // across * CHUNK, q % across * LANES
        p = place[q]
        tile = total[r:r + CHUNK, c:c + LANES]

        @pl.when(p < chunks)
        def _():
            keep_ref[pl.ds(pl.multiple_of(p * CHUNK, CHUNK), CHUNK), :] = tile

        @pl.when(p >= chunks)
        def _():
            send_ref[pl.ds(pl.multiple_of((p - chunks) * CHUNK, CHUNK), CHUNK), :] = tile

    ends = jnp.concatenate(
        [
            (vec[r:r + 1, :] + vec[r + 1:r + 2, :])[:, c * LANES:(c + 1) * LANES]
            for r in (2, 0)
            for c in range(across)
        ],
        axis=0,
    )
    keep_ref[chunks * CHUNK:, :] = ends
    send_ref[chunks * CHUNK:, :] = ends


def gradients(place, slots, dense, grad, grad_t, weight, pieces, tables):
    blocks = dense.shape[0]
    width = grad.shape[1]
    depth = weight.shape[0]
    count = 9 * blocks
    message = (width * depth // (2 * LANES) + 8, LANES)
    return pl.pallas_call(
        functools.partial(gradients_body, pieces),
        grid_spec=pltpu.PrefetchScalarGridSpec(
            num_scalar_prefetch=2,
            grid=(1,),
            in_specs=[pl.BlockSpec(memory_space=pl.ANY)]
            + [fixed(a.shape) for a in (grad, grad_t, weight)]
            + [pl.BlockSpec(memory_space=pl.ANY)] * len(tables),
            out_specs=[
                fixed((count, 1, BLK)), fixed((blocks, 1, BLK)), fixed(message), fixed(message)
            ],
            scratch_shapes=[
                pltpu.VMEM((count, BLK, depth), bf16),
                pltpu.VMEM(dense.shape, f32),
                pltpu.VMEM(grad.shape[:1] + (depth,), bf16),
                pltpu.VMEM((2, BLK, NBL * BLK), f32),
                pltpu.VMEM((blocks, BLK, depth), bf16),
                pltpu.VMEM((16, depth), f32),
                pltpu.VMEM((width, depth), f32),
                pltpu.SemaphoreType.DMA((len(tables) + blocks,)),
            ],
        ),
        out_shape=[
            jax.ShapeDtypeStruct((count, 1, BLK), f32),
            jax.ShapeDtypeStruct((blocks, 1, BLK), f32),
            jax.ShapeDtypeStruct(message, f32),
            jax.ShapeDtypeStruct(message, f32),
        ],
        compiler_params=pltpu.CompilerParams(
            dimension_semantics=("arbitrary",), vmem_limit_bytes=60 * MIB
        ),
        cost_estimate=pl.CostEstimate(flops=0, bytes_accessed=0, transcendentals=0),
        name="gradients",
    )(place, slots, dense, grad, grad_t, weight, *tables)


def columns_of(row):
    return jnp.broadcast_to(row, (LANES, row.shape[1])).T


def finish_weight_body(scale, place, near_ref, away_ref, vec_ref, src_ref, dst_ref, weight_ref,
                       out_ref, grad_src_ref, grad_dst_ref, total):
    across = total.shape[1] // LANES
    chunks = near_ref.shape[0]
    for q in range(2 * chunks):
        r, c = q // across * CHUNK, q % across * LANES
        p = place[q]
        at = lax.rem(p, chunks)
        tile = jnp.where(p < chunks, near_ref[at].astype(f32), away_ref[at].astype(f32))
        total[r:r + CHUNK, c:c + LANES] = tile
    rows = [
        jnp.concatenate([vec_ref[v * across + c][None] for c in range(across)], axis=1)
        for v in range(2)
    ]
    full = total[...]
    for ref, row in zip((src_ref, dst_ref), rows):
        full = full + jnp.concatenate([columns_of(ref[...])] * across, axis=1) * row
    out_ref[...] = full.T * scale
    terms = [two_terms(rows[0], 0, 16), two_terms(rows[1], 2, 16)]
    for v, row in enumerate(rows):
        main = row.astype(bf16).astype(f32)
        last = row - main
        last = last - last.astype(bf16).astype(f32)
        at = lax.broadcasted_iota(jnp.int32, (16, row.shape[1]), 0)
        terms.append(jnp.where(at == 4 + v, last, 0.0))
    lhs = sum(terms[1:], terms[0]).astype(bf16)
    out = jnp.dot(lhs, weight_ref[...], preferred_element_type=f32) * scale
    grad_src_ref[...] = (out[0:1, :] + out[1:2, :] + out[4:5, :]).reshape(out.shape[1])
    grad_dst_ref[...] = (out[2:3, :] + out[3:4, :] + out[5:6, :]).reshape(out.shape[1])


def finish_weight(place, near, away, vec, src, dst, weight, scale):
    depth, width = weight.shape
    whole = lambda shape: pl.BlockSpec(shape, lambda i, p: (0,) * len(shape))
    args = (near, away, vec, src, dst, weight)
    return pl.pallas_call(
        functools.partial(finish_weight_body, scale),
        grid_spec=pltpu.PrefetchScalarGridSpec(
            num_scalar_prefetch=1,
            grid=(1,),
            in_specs=[whole(a.shape) for a in args],
            out_specs=[whole((depth, width)), whole((width,)), whole((width,))],
            scratch_shapes=[pltpu.VMEM((width, depth), f32)],
        ),
        out_shape=[
            jax.ShapeDtypeStruct((depth, width), f32),
            jax.ShapeDtypeStruct((width,), f32),
            jax.ShapeDtypeStruct((width,), f32),
        ],
        compiler_params=pltpu.CompilerParams(
            dimension_semantics=("arbitrary",), vmem_limit_bytes=60 * MIB
        ),
        name="finish_weight",
    )(place, *args)


def finish_features_body(own_ref, twin_ref, far_ref, above_ref, below_ref, du_ref, sums_ref,
                         src_ref, dst_ref, weight_ref, out_ref, src_cols, dst_cols):
    @pl.when(pl.program_id(0) == 0)
    def _():
        src_cols[...] = columns_of(src_ref[...])
        dst_cols[...] = columns_of(dst_ref[...])

    width = own_ref.shape[1]
    for k in range(du_ref.shape[0]):
        total = own_ref[k] + twin_ref[k].astype(f32) + far_ref[k].astype(f32)
        sums = sums_ref[k]
        for ref in (above_ref, below_ref):
            total = total + ref[k, :width].astype(f32)
            carried = ref[k, width:width + 16].astype(f32)
            sums = sums + carried[0:1] + carried[1:2] + carried[2:3]
        total = total + src_cols[...] * du_ref[k] + dst_cols[...] * sums
        out_ref[k * BLK:(k + 1) * BLK, :] = lax.dot_general(
            total.T.astype(bf16), weight_ref[...], (((1,), (1,)), ((), ())),
            preferred_element_type=f32,
        ).astype(bf16)


def finish_features(own, twin, far, above, below, du, sums, src, dst, weight):
    blocks = du.shape[0]
    depth, width = weight.shape
    group = blocks // 2
    tile = lambda array: pl.BlockSpec((group,) + array.shape[1:], lambda b: (b, 0, 0))
    line = pl.BlockSpec((1, width), lambda b: (0, 0))
    arrays = [own, twin, far, above, below, du, sums]
    return pl.pallas_call(
        finish_features_body,
        grid=(blocks // group,),
        in_specs=[tile(array) for array in arrays] + [line] * 2
        + [pl.BlockSpec(weight.shape, lambda b: (0, 0))],
        out_specs=pl.BlockSpec((group * BLK, depth), lambda b: (b, 0)),
        scratch_shapes=[pltpu.VMEM((width, BLK), f32)] * 2,
        out_shape=jax.ShapeDtypeStruct((blocks * BLK, depth), bf16),
        compiler_params=pltpu.CompilerParams(
            dimension_semantics=("arbitrary",), vmem_limit_bytes=60 * MIB
        ),
        cost_estimate=pl.CostEstimate(
            flops=6 * 10**9, bytes_accessed=MIB, transcendentals=0
        ),
        name="finish_features",
    )(*arrays, src, dst, weight)


def ring(axis, low, count, offset):
    size = lax.axis_size(axis)
    turned = lambda i: ((i >> low) + offset) % count - (i >> low) % count
    return [(i, i + (turned(i) << low)) for i in range(size)]


def turned(array, stage):
    axis, low, count = stage
    return [lax.ppermute(array, axis, ring(axis, low, count, k)) for k in range(1, count)]


def three_terms(array, axis):
    main = array.astype(bf16)
    rest = array - main.astype(f32)
    second = rest.astype(bf16)
    last = (rest - second.astype(f32)).astype(bf16)
    return jnp.concatenate([main, second, last], axis=axis)


def lowered(array, ends):
    return jnp.concatenate(
        [array.astype(bf16), three_terms(ends, 0), jnp.zeros(ends.shape, bf16)]
    )


def raised(terms):
    tail = terms.shape[0] // 4
    return terms[:tail] + terms[tail:2 * tail] + terms[2 * tail:3 * tail]


def summed(array, stage):
    first, across, last = (t.astype(f32) for t in turned(array, stage))
    return (array.astype(f32) + across) + (first + last)


def scattered(array, stage, tail):
    axis, start, count = stage
    rows = (array.shape[0] - tail) // count
    ends = array[count * rows:]
    own = array[:rows]
    came = []
    for k in range(1, count):
        message = lowered(array[k * rows:(k + 1) * rows], ends)
        came.append(lax.ppermute(message, axis, ring(axis, start, count, k)).astype(f32))
    first, across, last = came
    matrix = (own + across[:rows]) + (first[:rows] + last[:rows])
    vector = (ends + raised(across[rows:])) + (raised(first[rows:]) + raised(last[rows:]))
    return jnp.concatenate([matrix, vector])


def after(array, *others):
    return lax.optimization_barrier((array, *others))[0]


def crossed(first, second, size):
    return [(a * size + c, b * size + d) for a, b in first for c, d in second]


def places(stages, sign):
    chunk = jnp.arange(math.prod(n for _, _, n in stages), dtype=jnp.int32)
    place, stride = jnp.zeros_like(chunk), 1
    for axis, low, count in stages[::-1]:
        here = (lax.axis_index(axis) >> low) % count
        place = place + (sign * (chunk // stride % count - here)) % count * stride
        stride = stride * count
    return place


def on_device(features, weight, attn_src, attn_dst, upstream, scores, neighbour_lists, edge_index):
    rows, depth = features.shape
    width = weight.shape[1]
    blocks = rows // BLK
    size_x = lax.axis_size("gx")
    size_y = lax.axis_size("gy")
    here_x = lax.axis_index("gx")
    here_y = lax.axis_index("gy")
    twin = [(i, i ^ 1) for i in range(size_x)]
    far = [(i, (((i + 1) ^ 1) - 1) % size_x) for i in range(size_x)]
    up = [(i, (i + 1) % size_y) for i in range(size_y)]
    down = [(i, (i - 1) % size_y) for i in range(size_y)]

    owner = neighbour_lists // blocks
    owner_x, owner_y = owner // size_y, owner % size_y
    part_x = jnp.where(owner_x == here_x, 0, jnp.where(owner_x // 2 == here_x // 2, 1, 2))
    part_y = jnp.where(owner_y == here_y, 0, jnp.where(owner_y == (here_y + 1) % size_y, 1, 2))
    slots = (part_x * 3 + part_y) * blocks + neighbour_lists % blocks

    own = features.reshape(blocks, BLK, depth)
    above = lax.ppermute(own, "gy", down)
    below = lax.ppermute(own, "gy", up)
    away = lax.ppermute(own, "gx", far)
    from_y = [lax.ppermute(own, ("gx", "gy"), crossed(far, way, size_y)) for way in (down, up)]
    dense, acc_own, twin_o, acc_twin, far_o, acc_far, grad_t = spread(
        slots, scores.T, edge_index.T, upstream
    )
    away, *from_y, dense, acc_own, acc_twin, acc_far, own_late = lax.optimization_barrier(
        (away, *from_y, dense, acc_own, acc_twin, acc_far, own)
    )
    across = lax.ppermute(own_late, "gx", twin)
    above, below, across = lax.optimization_barrier((above, below, across))
    sides = [across] + [lax.ppermute(t, "gx", twin) for t in (above, below)]
    from_far = lax.ppermute(acc_far, "gx", far)
    from_twin = lax.ppermute(acc_twin, "gx", twin)
    tables = [own, above, below, *sides, away, *from_y]
    pieces = tuple((k * blocks, blocks) for k in range(9))

    core, along_y, along_z = ("gx", 0, 2), ("gy", 0, 4), ("gx", 1, size_x // 2)
    stages = (core, along_y)
    sums, du, keep, send = gradients(
        places(stages, 1), slots, dense, upstream, grad_t, weight, pieces, tables
    )
    sums, du, keep, send, from_far, from_twin = lax.optimization_barrier(
        (sums, du, keep, send, from_far, from_twin)
    )
    sums = sums.reshape(3, 3, blocks, 1, BLK)
    part = keep + lax.ppermute(send, "gx", twin)

    part, sums = lax.optimization_barrier((part, sums))
    sums = sums[0] + lax.ppermute(sums[1], "gx", twin) + lax.ppermute(sums[2], "gx", far)

    def column(k):
        rows = slice((k - 1) * blocks, k * blocks)
        total = acc_own[k * blocks:(k + 1) * blocks] + from_twin[rows].astype(f32)
        total = total + from_far[rows].astype(f32)
        terms = jnp.pad(three_terms(sums[k], 1), ((0, 0), (0, 13), (0, 0)))
        return jnp.concatenate([total.astype(bf16), terms], axis=1)

    part = scattered(part, along_y, 8)
    part, sums = lax.optimization_barrier((part, sums))
    to_above, to_below = column(1), column(2)
    from_below = lax.ppermute(to_above, "gy", up)
    from_above = lax.ppermute(to_below, "gy", down)
    part = summed(part, along_z)
    part, far_o, twin_o = lax.optimization_barrier((part, far_o, twin_o))
    from_far_o = lax.ppermute(far_o, "gx", far)
    from_twin_o = lax.ppermute(twin_o, "gx", twin)
    part, from_below, from_above, from_far_o, from_twin_o = lax.optimization_barrier(
        (part, from_below, from_above, from_far_o, from_twin_o)
    )
    part = summed(lowered(part[:CHUNK], part[CHUNK:]), ("gy", 2, size_y // 4))
    vec = raised(part[CHUNK:])
    part = part[:CHUNK].astype(bf16)
    part, du = lax.optimization_barrier((part, du))
    part = part[None]
    part = jnp.concatenate([part] + turned(part, along_y))
    src, dst = attn_src[None], attn_dst[None]
    grad_features = finish_features(
        acc_own, from_twin_o, from_far_o, from_above, from_below, du, sums[0], src, dst, weight
    )
    part, grad_features = lax.optimization_barrier((part, grad_features))
    scale = 1.0 / math.sqrt(rows * size_x * size_y)
    grad_weight, grad_src, grad_dst = finish_weight(
        places(stages, -1), part, lax.ppermute(part, "gx", twin), vec, src, dst, weight, scale
    )
    return (grad_features, grad_weight, grad_src, grad_dst)


def solution(mesh):
    rows = P(("gx", "gy"), None)
    return jax.shard_map(
        on_device,
        mesh=mesh,
        in_specs=(rows, P(), P(), P(), rows, rows, rows, rows),
        out_specs=(rows, P(), P(), P()),
        check_vma=False,
    )
```

```python
import functools
import math

import jax
import jax.numpy as jnp
from jax import lax
from jax.experimental import pallas as pl
from jax.experimental.pallas import tpu as pltpu
from jax.sharding import PartitionSpec as P

BLK = 128
NBL = 16
WIDE = 256
HALVES = NBL * BLK // WIDE
LANES = 128
CHUNK = 256
JOINED = 4
MIB = 1 << 20

f32 = jnp.float32
bf16 = jnp.bfloat16


def spread_body(edges, slots, score_ref, index_ref, grad_ref, dense_ref, own_ref, twin_o_ref,
                twin_ref, far_o_ref, far_ref, grad_t, left_scr, right_scr, low_scr, high_scr, main_scr, rest_scr, dense,
                acc, sem):
    blocks = dense.shape[0]
    pad = ((0, LANES - edges), (0, 0))
    lanes = lax.broadcasted_iota(jnp.int32, (edges, LANES), 1).astype(f32).astype(bf16)
    halves = lax.broadcasted_iota(jnp.int32, (HALVES, LANES), 0).astype(f32)
    one = jnp.ones((edges, LANES), bf16)
    none = jnp.zeros((edges, LANES), bf16)
    tail = jnp.zeros((LANES - edges, WIDE), bf16)
    acc[...] = jnp.zeros_like(acc)
    score = score_ref[...]
    logit = jnp.where(score > 0, score, 0.2 * score)
    expo = jnp.exp(logit - jnp.max(logit, axis=0, keepdims=True))
    alpha = expo / jnp.sum(expo, axis=0, keepdims=True)
    main = alpha.astype(bf16).astype(f32)
    rest = (alpha - main).astype(bf16).astype(f32)
    index = index_ref[...]
    low_scr[...] = (index % WIDE).astype(f32)
    high = jnp.pad((index // WIDE).astype(f32), pad, constant_values=-1.0)
    main = jnp.pad(jnp.where(score > 0, main, -main), pad)
    rest = jnp.pad(jnp.where(score > 0, rest, -rest), pad)
    for b in range(blocks):
        nodes = slice(b * BLK, (b + 1) * BLK)
        high_scr[nodes, :] = high[:, nodes].T
        main_scr[nodes, :] = main[:, nodes].T
        rest_scr[nodes, :] = rest[:, nodes].T
        grad_t[b] = grad_ref[nodes, :].T

    def out_copy(step):
        return pltpu.make_async_copy(dense.at[step], dense_ref.at[step], sem.at[step])

    def block(step, carry):
        nodes = pl.ds(pl.multiple_of(step * BLK, BLK), BLK)
        low = low_scr[:, nodes]
        high, main, rest = high_scr[nodes, :], main_scr[nodes, :], rest_scr[nodes, :]
        for i in range(BLK):
            here = jnp.broadcast_to(high[i:i + 1, :], (HALVES, LANES)) == halves
            lhs = jnp.concatenate(
                [
                    jnp.where(here, jnp.broadcast_to(term[i:i + 1, :], (HALVES, LANES)), 0.0)
                    for term in (main, rest)
                ],
                axis=0,
            ).astype(bf16)
            column = jnp.broadcast_to(low[:, i:i + 1], (edges, LANES)).astype(bf16)
            rhs = jnp.concatenate(
                [jnp.where(column == lanes + LANES * c, one, none) for c in range(WIDE // LANES)],
                axis=1,
            )
            rhs = jnp.concatenate([rhs, tail], axis=0)
            out = jnp.dot(lhs, rhs, preferred_element_type=f32)
            left_scr[2 * HALVES * i:2 * HALVES * (i + 1), :] = out[:, :LANES]
            right_scr[2 * HALVES * i:2 * HALVES * (i + 1), :] = out[:, LANES:]
        for s in range(NBL):
            scr = (left_scr, right_scr)[s % 2]
            main = scr[pl.ds(s // 2, BLK, stride=2 * HALVES), :]
            rest = scr[pl.ds(HALVES + s // 2, BLK, stride=2 * HALVES), :]
            dense[step, :, s * BLK:(s + 1) * BLK] = main + rest
            low = jnp.abs(main).astype(bf16)
            term = jnp.dot(grad_t[step], low, preferred_element_type=f32)[None]
            acc[pl.ds(slots[step, s], 1)] += term
        out_copy(step).start()
        return carry

    lax.fori_loop(0, blocks, block, 0)
    per = own_ref.shape[0]

    def cast(k, carry):
        own_ref[pl.ds(k, 1)] = acc[pl.ds(2 * per + k, 1)]
        return carry

    def cast_own(k, carry):
        twin_o_ref[pl.ds(k, 1)] = acc[pl.ds(k, 1)].astype(bf16)
        far_o_ref[pl.ds(k, 1)] = acc[pl.ds(per + k, 1)].astype(bf16)
        return carry

    def cast_sides(k, carry):
        twin_ref[pl.ds(k, 1)] = acc[pl.ds(blocks + k, 1)].astype(bf16)
        far_ref[pl.ds(k, 1)] = acc[pl.ds(per + blocks + k, 1)].astype(bf16)
        return carry

    lax.fori_loop(0, per, cast, 0)
    lax.fori_loop(0, blocks, cast_own, 0)
    lax.fori_loop(0, per - blocks, cast_sides, 0)
    lax.fori_loop(0, blocks, lambda step, carry: (out_copy(step).wait(), carry)[1], 0)


def fixed(shape):
    return pl.BlockSpec(shape, lambda *_: (0,) * len(shape), pipeline_mode=pl.Buffered(1))


def spread(slots, scores, index, grad):
    edges, rows = scores.shape
    blocks = rows // BLK
    width = grad.shape[1]
    per = 3 * blocks
    away = [(blocks, width, BLK), (2 * blocks, width, BLK)]
    sums = [(per, width, BLK)] + away + away + [(blocks, width, BLK)]
    types = [f32] + [bf16] * 5
    dense = (blocks, BLK, NBL * BLK)
    return pl.pallas_call(
        functools.partial(spread_body, edges),
        grid_spec=pltpu.PrefetchScalarGridSpec(
            num_scalar_prefetch=1,
            grid=(1,),
            in_specs=[fixed(scores.shape), fixed(index.shape), fixed(grad.shape)],
            out_specs=[pl.BlockSpec(memory_space=pl.ANY)] + [fixed(shape) for shape in sums],
            scratch_shapes=[
                pltpu.VMEM((2 * HALVES * (BLK + 1), LANES), f32),
                pltpu.VMEM((2 * HALVES * (BLK + 1), LANES), f32),
                pltpu.VMEM((edges, rows), f32),
                pltpu.VMEM((rows, LANES), f32),
                pltpu.VMEM((rows, LANES), f32),
                pltpu.VMEM((rows, LANES), f32),
                pltpu.VMEM(dense, f32),
                pltpu.VMEM((3 * per, width, BLK), f32),
                pltpu.SemaphoreType.DMA((blocks,)),
            ],
        ),
        out_shape=[jax.ShapeDtypeStruct(dense, f32)]
        + [jax.ShapeDtypeStruct(*pair) for pair in zip(sums, types)],
        compiler_params=pltpu.CompilerParams(
            dimension_semantics=("arbitrary",), vmem_limit_bytes=60 * MIB
        ),
        cost_estimate=pl.CostEstimate(flops=0, bytes_accessed=0, transcendentals=0),
        name="spread",
    )((slots + 2 * per) % (3 * per), scores, index, grad)


def two_terms(row, first, rows):
    at = lax.broadcasted_iota(jnp.int32, (rows, row.shape[1]), 0)
    row = jnp.broadcast_to(row, at.shape)
    main = row.astype(bf16).astype(f32)
    return jnp.where(at == first, main, jnp.where(at == first + 1, row - main, 0.0))


def gradients_body(pieces, place, slots, dense_ref, grad_ref, grad_t, weight_ref, *rest):
    count = len(pieces)
    tables = rest[:count]
    sums_ref, du_ref, keep_ref, send_ref = rest[count:count + 4]
    table, dense, probe, prod, mixed, vec, total, sem = rest[count + 4:]
    blocks = dense.shape[0]
    depth = table.shape[2]
    abreast = prod.shape[0]

    def dense_copy(step):
        return pltpu.make_async_copy(dense_ref.at[step], dense.at[step], sem.at[count + step])

    copies = [
        pltpu.make_async_copy(t, table.at[pl.ds(first, size)], sem.at[k])
        for k, (t, (first, size)) in enumerate(zip(tables, pieces))
    ]
    for copy in copies:
        copy.start()
    lax.fori_loop(0, blocks, lambda step, carry: (dense_copy(step).start(), carry)[1], 0)
    sums_ref[...] = jnp.zeros_like(sums_ref)
    vec[...] = jnp.zeros_like(vec)

    def project(step, carry):
        nodes = pl.ds(pl.multiple_of(step * BLK, BLK), BLK)
        probe[nodes, :] = lax.dot_general(
            grad_ref[nodes, :], weight_ref[...], (((1,), (1,)), ((), ())),
            preferred_element_type=f32,
        ).astype(bf16)
        return carry

    lax.fori_loop(0, blocks, project, 0)
    for copy in copies:
        copy.wait()

    def group(first, carry):
        steps = [first * abreast + u for u in range(abreast)]
        means = []
        for u, step in enumerate(steps):
            dense_copy(step).wait()
            row = probe[pl.ds(pl.multiple_of(step * BLK, BLK), BLK), :]
            inner = jnp.zeros((BLK, BLK), f32)
            sized = jnp.zeros((BLK, BLK), f32)
            for s in range(NBL):
                cols = slice(s * BLK, (s + 1) * BLK)
                d = lax.dot_general(
                    row, table[slots[step, s]], (((1,), (1,)), ((), ())),
                    preferred_element_type=f32,
                )
                prod[u, :, cols] = d
                a = jnp.abs(dense[step, :, cols])
                inner = inner + a * d
                sized = sized + a
            means.append(
                jnp.sum(inner, axis=1, keepdims=True) / jnp.sum(sized, axis=1, keepdims=True)
            )
        for u, step in enumerate(steps):
            du = jnp.zeros((BLK, BLK), f32)
            mix = jnp.zeros((BLK + 16, depth), f32)
            for first in range(0, NBL, JOINED):
                lhs, rhs = [], []
                for s in range(first, first + JOINED):
                    cols = slice(s * BLK, (s + 1) * BLK)
                    a = dense[step, :, cols]
                    dz = jnp.maximum(a, -0.2 * a) * (prod[u, :, cols] - means[u])
                    du = du + dz
                    slot = slots[step, s]
                    sums = jnp.sum(dz, axis=0, keepdims=True)
                    sums_ref[pl.ds(slot, 1)] += sums[None]
                    lhs.append(
                        jnp.concatenate(
                            [jnp.abs(a).astype(bf16), two_terms(sums, 0, 16).astype(bf16)], axis=0
                        )
                    )
                    rhs.append(table[slot])
                mix = mix + jnp.dot(
                    jnp.concatenate(lhs, axis=1), jnp.concatenate(rhs, axis=0),
                    preferred_element_type=f32,
                )
            row = jnp.broadcast_to(jnp.sum(du, axis=1, keepdims=True), (BLK, BLK)).T[0:1, :]
            du_ref[pl.ds(step, 1)] = row[None]
            mixed[step] = mix[:BLK].astype(bf16)
            vec[...] += mix[BLK:] + jnp.dot(
                two_terms(row, 2, 16).astype(bf16), table[step], preferred_element_type=f32
            )
        return carry

    lax.fori_loop(0, blocks // abreast, group, 0)
    lhs = jnp.concatenate([grad_t[b] for b in range(blocks)], axis=1)
    rhs = mixed[...].reshape(blocks * BLK, depth)
    total[...] = jnp.dot(lhs, rhs, preferred_element_type=f32)
    across = depth // LANES
    chunks = keep_ref.shape[0] // CHUNK
    for q in range(2 * chunks):
        r, c = q // across * CHUNK, q % across * LANES
        p = place[q]
        tile = total[r:r + CHUNK, c:c + LANES]

        @pl.when(p < chunks)
        def _():
            keep_ref[pl.ds(pl.multiple_of(p * CHUNK, CHUNK), CHUNK), :] = tile

        @pl.when(p >= chunks)
        def _():
            send_ref[pl.ds(pl.multiple_of((p - chunks) * CHUNK, CHUNK), CHUNK), :] = tile

    ends = jnp.concatenate(
        [
            (vec[r:r + 1, :] + vec[r + 1:r + 2, :])[:, c * LANES:(c + 1) * LANES]
            for r in (2, 0)
            for c in range(across)
        ],
        axis=0,
    )
    keep_ref[chunks * CHUNK:, :] = ends
    send_ref[chunks * CHUNK:, :] = ends


def gradients(place, slots, dense, grad, grad_t, weight, pieces, tables):
    blocks = dense.shape[0]
    width = grad.shape[1]
    depth = weight.shape[0]
    count = 9 * blocks
    message = (width * depth // (2 * LANES) + 8, LANES)
    return pl.pallas_call(
        functools.partial(gradients_body, pieces),
        grid_spec=pltpu.PrefetchScalarGridSpec(
            num_scalar_prefetch=2,
            grid=(1,),
            in_specs=[pl.BlockSpec(memory_space=pl.ANY)]
            + [fixed(a.shape) for a in (grad, grad_t, weight)]
            + [pl.BlockSpec(memory_space=pl.ANY)] * len(tables),
            out_specs=[
                fixed((count, 1, BLK)), fixed((blocks, 1, BLK)), fixed(message), fixed(message)
            ],
            scratch_shapes=[
                pltpu.VMEM((count, BLK, depth), bf16),
                pltpu.VMEM(dense.shape, f32),
                pltpu.VMEM(grad.shape[:1] + (depth,), bf16),
                pltpu.VMEM((2, BLK, NBL * BLK), f32),
                pltpu.VMEM((blocks, BLK, depth), bf16),
                pltpu.VMEM((16, depth), f32),
                pltpu.VMEM((width, depth), f32),
                pltpu.SemaphoreType.DMA((len(tables) + blocks,)),
            ],
        ),
        out_shape=[
            jax.ShapeDtypeStruct((count, 1, BLK), f32),
            jax.ShapeDtypeStruct((blocks, 1, BLK), f32),
            jax.ShapeDtypeStruct(message, f32),
            jax.ShapeDtypeStruct(message, f32),
        ],
        compiler_params=pltpu.CompilerParams(
            dimension_semantics=("arbitrary",), vmem_limit_bytes=60 * MIB
        ),
        cost_estimate=pl.CostEstimate(flops=0, bytes_accessed=0, transcendentals=0),
        name="gradients",
    )(place, slots, dense, grad, grad_t, weight, *tables)


def columns_of(row):
    return jnp.broadcast_to(row, (LANES, row.shape[1])).T


def finish_weight_body(scale, place, near_ref, away_ref, vec_ref, src_ref, dst_ref, weight_ref,
                       out_ref, grad_src_ref, grad_dst_ref, total):
    across = total.shape[1] // LANES
    chunks = near_ref.shape[0]
    for q in range(2 * chunks):
        r, c = q // across * CHUNK, q % across * LANES
        p = place[q]
        at = lax.rem(p, chunks)
        tile = jnp.where(p < chunks, near_ref[at].astype(f32), away_ref[at].astype(f32))
        total[r:r + CHUNK, c:c + LANES] = tile
    rows = [
        jnp.concatenate([vec_ref[v * across + c][None] for c in range(across)], axis=1)
        for v in range(2)
    ]
    full = total[...]
    for ref, row in zip((src_ref, dst_ref), rows):
        full = full + jnp.concatenate([columns_of(ref[...])] * across, axis=1) * row
    out_ref[...] = full.T * scale
    terms = [two_terms(rows[0], 0, 16), two_terms(rows[1], 2, 16)]
    for v, row in enumerate(rows):
        main = row.astype(bf16).astype(f32)
        last = row - main
        last = last - last.astype(bf16).astype(f32)
        at = lax.broadcasted_iota(jnp.int32, (16, row.shape[1]), 0)
        terms.append(jnp.where(at == 4 + v, last, 0.0))
    lhs = sum(terms[1:], terms[0]).astype(bf16)
    out = jnp.dot(lhs, weight_ref[...], preferred_element_type=f32) * scale
    grad_src_ref[...] = (out[0:1, :] + out[1:2, :] + out[4:5, :]).reshape(out.shape[1])
    grad_dst_ref[...] = (out[2:3, :] + out[3:4, :] + out[5:6, :]).reshape(out.shape[1])


def finish_weight(place, near, away, vec, src, dst, weight, scale):
    depth, width = weight.shape
    whole = lambda shape: pl.BlockSpec(shape, lambda i, p: (0,) * len(shape))
    args = (near, away, vec, src, dst, weight)
    return pl.pallas_call(
        functools.partial(finish_weight_body, scale),
        grid_spec=pltpu.PrefetchScalarGridSpec(
            num_scalar_prefetch=1,
            grid=(1,),
            in_specs=[whole(a.shape) for a in args],
            out_specs=[whole((depth, width)), whole((width,)), whole((width,))],
            scratch_shapes=[pltpu.VMEM((width, depth), f32)],
        ),
        out_shape=[
            jax.ShapeDtypeStruct((depth, width), f32),
            jax.ShapeDtypeStruct((width,), f32),
            jax.ShapeDtypeStruct((width,), f32),
        ],
        compiler_params=pltpu.CompilerParams(
            dimension_semantics=("arbitrary",), vmem_limit_bytes=20 * MIB
        ),
        name="finish_weight",
    )(place, *args)


def finish_features_body(own_ref, twin_ref, far_ref, above_ref, below_ref, du_ref, sums_ref,
                         src_ref, dst_ref, weight_ref, out_ref, src_cols, dst_cols):
    @pl.when(pl.program_id(0) == 0)
    def _():
        src_cols[...] = columns_of(src_ref[...])
        dst_cols[...] = columns_of(dst_ref[...])

    width = own_ref.shape[1]
    for k in range(du_ref.shape[0]):
        total = own_ref[k] + twin_ref[k].astype(f32) + far_ref[k].astype(f32)
        sums = sums_ref[k]
        for ref in (above_ref, below_ref):
            total = total + ref[k, :width].astype(f32)
            carried = ref[k, width:width + 16].astype(f32)
            sums = sums + carried[0:1] + carried[1:2] + carried[2:3]
        total = total + src_cols[...] * du_ref[k] + dst_cols[...] * sums
        out_ref[k * BLK:(k + 1) * BLK, :] = lax.dot_general(
            total.T.astype(bf16), weight_ref[...], (((1,), (1,)), ((), ())),
            preferred_element_type=f32,
        ).astype(bf16)


def finish_features(own, twin, far, above, below, du, sums, src, dst, weight):
    blocks = du.shape[0]
    depth, width = weight.shape
    group = blocks // 2
    tile = lambda array: pl.BlockSpec((group,) + array.shape[1:], lambda b: (b, 0, 0))
    line = pl.BlockSpec((1, width), lambda b: (0, 0))
    arrays = [own, twin, far, above, below, du, sums]
    return pl.pallas_call(
        finish_features_body,
        grid=(blocks // group,),
        in_specs=[tile(array) for array in arrays] + [line] * 2
        + [pl.BlockSpec(weight.shape, lambda b: (0, 0))],
        out_specs=pl.BlockSpec((group * BLK, depth), lambda b: (b, 0)),
        scratch_shapes=[pltpu.VMEM((width, BLK), f32)] * 2,
        out_shape=jax.ShapeDtypeStruct((blocks * BLK, depth), bf16),
        compiler_params=pltpu.CompilerParams(
            dimension_semantics=("arbitrary",), vmem_limit_bytes=20 * MIB
        ),
        cost_estimate=pl.CostEstimate(
            flops=6 * 10**9, bytes_accessed=MIB, transcendentals=0
        ),
        name="finish_features",
    )(*arrays, src, dst, weight)


def ring(axis, low, count, offset):
    size = lax.axis_size(axis)
    turned = lambda i: ((i >> low) + offset) % count - (i >> low) % count
    return [(i, i + (turned(i) << low)) for i in range(size)]


def turned(array, stage):
    axis, low, count = stage
    return [lax.ppermute(array, axis, ring(axis, low, count, k)) for k in range(1, count)]


def three_terms(array, axis):
    main = array.astype(bf16)
    rest = array - main.astype(f32)
    second = rest.astype(bf16)
    last = (rest - second.astype(f32)).astype(bf16)
    return jnp.concatenate([main, second, last], axis=axis)


def lowered(array, ends):
    return jnp.concatenate(
        [array.astype(bf16), three_terms(ends, 0), jnp.zeros(ends.shape, bf16)]
    )


def raised(terms):
    tail = terms.shape[0] // 4
    return terms[:tail] + terms[tail:2 * tail] + terms[2 * tail:3 * tail]


def summed(array, stage):
    first, across, last = (t.astype(f32) for t in turned(array, stage))
    return (array.astype(f32) + across) + (first + last)


def scattered(array, stage, tail):
    axis, start, count = stage
    rows = (array.shape[0] - tail) // count
    ends = array[count * rows:]
    own = array[:rows]
    came = []
    for k in range(1, count):
        message = lowered(array[k * rows:(k + 1) * rows], ends)
        came.append(lax.ppermute(message, axis, ring(axis, start, count, k)).astype(f32))
    first, across, last = came
    matrix = (own + across[:rows]) + (first[:rows] + last[:rows])
    vector = (ends + raised(across[rows:])) + (raised(first[rows:]) + raised(last[rows:]))
    return jnp.concatenate([matrix, vector])


def after(array, *others):
    return lax.optimization_barrier((array, *others))[0]


def crossed(first, second, size):
    return [(a * size + c, b * size + d) for a, b in first for c, d in second]


def places(stages, sign):
    chunk = jnp.arange(math.prod(n for _, _, n in stages), dtype=jnp.int32)
    place, stride = jnp.zeros_like(chunk), 1
    for axis, low, count in stages[::-1]:
        here = (lax.axis_index(axis) >> low) % count
        place = place + (sign * (chunk // stride % count - here)) % count * stride
        stride = stride * count
    return place


def on_device(features, weight, attn_src, attn_dst, upstream, scores, neighbour_lists, edge_index):
    rows, depth = features.shape
    width = weight.shape[1]
    blocks = rows // BLK
    size_x = lax.axis_size("gx")
    size_y = lax.axis_size("gy")
    here_x = lax.axis_index("gx")
    here_y = lax.axis_index("gy")
    twin = [(i, i ^ 1) for i in range(size_x)]
    far = [(i, (((i + 1) ^ 1) - 1) % size_x) for i in range(size_x)]
    up = [(i, (i + 1) % size_y) for i in range(size_y)]
    down = [(i, (i - 1) % size_y) for i in range(size_y)]

    owner = neighbour_lists // blocks
    owner_x, owner_y = owner // size_y, owner % size_y
    part_x = jnp.where(owner_x == here_x, 0, jnp.where(owner_x // 2 == here_x // 2, 1, 2))
    part_y = jnp.where(owner_y == here_y, 0, jnp.where(owner_y == (here_y + 1) % size_y, 1, 2))
    slots = (part_x * 3 + part_y) * blocks + neighbour_lists % blocks

    own = features.reshape(blocks, BLK, depth)
    above = lax.ppermute(own, "gy", down)
    below = lax.ppermute(own, "gy", up)
    away = lax.ppermute(own, "gx", far)
    from_y = [lax.ppermute(own, ("gx", "gy"), crossed(far, way, size_y)) for way in (down, up)]
    dense, acc_own, twin_o, acc_twin, far_o, acc_far, grad_t = spread(
        slots, scores.T, edge_index.T, upstream
    )
    away, *from_y, dense, acc_own, acc_twin, acc_far, own_late = lax.optimization_barrier(
        (away, *from_y, dense, acc_own, acc_twin, acc_far, own)
    )
    across = lax.ppermute(own_late, "gx", twin)
    above, below, across = lax.optimization_barrier((above, below, across))
    sides = [across] + [lax.ppermute(t, "gx", twin) for t in (above, below)]
    from_far = lax.ppermute(acc_far, "gx", far)
    from_twin = lax.ppermute(acc_twin, "gx", twin)
    tables = [own, above, below, *sides, away, *from_y]
    pieces = tuple((k * blocks, blocks) for k in range(9))

    core, along_y, along_z = ("gx", 0, 2), ("gy", 0, 4), ("gx", 1, size_x // 2)
    stages = (core, along_y)
    sums, du, keep, send = gradients(
        places(stages, 1), slots, dense, upstream, grad_t, weight, pieces, tables
    )
    sums, du, keep, send, from_far, from_twin = lax.optimization_barrier(
        (sums, du, keep, send, from_far, from_twin)
    )
    sums = sums.reshape(3, 3, blocks, 1, BLK)
    part = keep + lax.ppermute(send, "gx", twin)

    part, sums = lax.optimization_barrier((part, sums))
    sums = sums[0] + lax.ppermute(sums[1], "gx", twin) + lax.ppermute(sums[2], "gx", far)

    def column(k):
        rows = slice((k - 1) * blocks, k * blocks)
        total = acc_own[k * blocks:(k + 1) * blocks] + from_twin[rows].astype(f32)
        total = total + from_far[rows].astype(f32)
        terms = jnp.pad(three_terms(sums[k], 1), ((0, 0), (0, 13), (0, 0)))
        return jnp.concatenate([total.astype(bf16), terms], axis=1)

    part = scattered(part, along_y, 8)
    part, sums = lax.optimization_barrier((part, sums))
    to_above, to_below = column(1), column(2)
    from_below = lax.ppermute(to_above, "gy", up)
    from_above = lax.ppermute(to_below, "gy", down)
    part = summed(part, along_z)
    part, far_o, twin_o = lax.optimization_barrier((part, far_o, twin_o))
    from_far_o = lax.ppermute(far_o, "gx", far)
    from_twin_o = lax.ppermute(twin_o, "gx", twin)
    part, from_below, from_above, from_far_o, from_twin_o = lax.optimization_barrier(
        (part, from_below, from_above, from_far_o, from_twin_o)
    )
    part = summed(lowered(part[:CHUNK], part[CHUNK:]), ("gy", 2, size_y // 4))
    vec = raised(part[CHUNK:])
    part = part[:CHUNK].astype(bf16)
    part, du = lax.optimization_barrier((part, du))
    part = part[None]
    part = jnp.concatenate([part] + turned(part, along_y))
    src, dst = attn_src[None], attn_dst[None]
    grad_features = finish_features(
        acc_own, from_twin_o, from_far_o, from_above, from_below, du, sums[0], src, dst, weight
    )
    part, grad_features = lax.optimization_barrier((part, grad_features))
    scale = 1.0 / math.sqrt(rows * size_x * size_y)
    grad_weight, grad_src, grad_dst = finish_weight(
        places(stages, -1), part, lax.ppermute(part, "gx", twin), vec, src, dst, weight, scale
    )
    return (grad_features, grad_weight, grad_src, grad_dst)


def solution(mesh):
    rows = P(("gx", "gy"), None)
    return jax.shard_map(
        on_device,
        mesh=mesh,
        in_specs=(rows, P(), P(), P(), rows, rows, rows, rows),
        out_specs=(rows, P(), P(), P()),
        check_vma=False,
    )
```
